32 devices in a mesh: expert: 16 (over z, y, x), tensor: 2 (over core).
Axes of the slice: x: 2, y: 2, z: 4, core: 2. Of those that a mesh axis runs over, the one named last changes fastest.
Arguments:
- grad_out: bfloat16 [8192, 3072], P('expert', 'tensor'), may hold values from -6 to 6
- hidden_in: bfloat16 [8192, 4096], P('expert', 'tensor')
- gate_prob: float32 [8192], P('expert'), may hold values from 0.1 to 1
- expert_ids: int32 [8192, 1], P('expert'), may hold values from 0 to 15; in each aligned block of 512 rows (0 to 511, 512 to 1023, ...) at most 64 rows name the same one
- w_down: bfloat16 [16, 4096, 3072], P('expert', 'tensor'), may hold values from -0.09375 to 0.09375
Outputs:
- grad_hidden: bfloat16 [8192, 4096], P('expert', 'tensor')
- grad_gate: float32 [8192], P('expert')
The draws below stay inside these ranges and needn't reach their ends.
Inputs may be any that keep to these rules, and one draw needn't show every extreme that they name: `expert_ids`: in each aligned block of 512 tokens no expert is named more than 64 times, a bound that some block reaches.
All inputs are finite; a program needn't handle non-finite values.
Results may differ from the reference program's by a relative error of at most 0.0049.
Values may be sent and summed in bfloat16 or wider, within the bound.
A program may use at most 64 MiB of HBM per device.

```python
import math
import jax
import jax.numpy as jnp
import numpy as np
from jax import lax

D = 3072
FF = 4096
TOK_DEV = 512
EXPERTS = 16
TOKENS = 8192
CAP = 64
N_EXPERT = 16


def draw_hidden_in(key, part):
    key = jax.random.fold_in(key, 7)
    first = jax.random.fold_in(key, 0)
    columns = jnp.arange(FF, dtype=jnp.float32)
    rising = jnp.exp(jnp.log(3.0) * columns / FF)[None, :]
    scale_all = 2.0 / jnp.sqrt(jnp.float32(FF))
    base = jax.random.normal(first, (TOKENS, FF), jnp.float32)
    values = base * rising * scale_all
    return values.astype(jnp.bfloat16)


def steps_of(key, dims, cuts, low, top_value):
    factor_of, own = 1.0, jax.random.fold_in(key, 6)
    for dim, shards_of in cuts:
        heights = jnp.exp(jax.random.uniform(jax.random.fold_in(own, dim), (shards_of,), jnp.float32, low / len(cuts), top_value / len(cuts)))
        factor_of = factor_of * jnp.repeat(heights, dims[dim] // shards_of).reshape([-1 if axis == dim else 1 for axis in range(len(dims))])
    return factor_of


def assign_block(rng, own, number, rows, count, top, most, skew):
    sequence = jax.random.permutation(rng, count)
    heavy_load, ordinary = portions_of(count, rows * top, most, skew, True), portions_of(count, rows * top, most, skew, False)
    places = jnp.arange(count)

    def named(tallies, offset_by):
        used = int((tallies > 0).sum())
        fixed = max(1, used // 4)
        moved = fixed + (places - fixed + offset_by * (used - fixed)) % max(1, count - fixed)
        return jnp.zeros((count,), jnp.int32).at[sequence[jnp.where(places < fixed, places, moved)]].set(jnp.asarray(tallies, jnp.int32))

    tallies = jnp.where(number % 4 == 0, named(heavy_load, number // 4), named(ordinary, number - number // 4 - 1))
    mixed = jax.random.permutation(jax.random.fold_in(own, 3), count)
    donor, sink = mixed[0:count // 2 * 2:2], mixed[1:count // 2 * 2:2]
    slack = jnp.minimum(tallies[donor] - 1, most - tallies[sink]) // 2
    slack = jnp.where((donor == sequence[0]) | (sink == sequence[0]) | (tallies[sink] == 0), 0, jnp.maximum(slack, 0))
    moved = jax.random.randint(jax.random.fold_in(own, 4), (count // 2,), 0, 1 << 20) % (slack + 1)
    tallies = tallies.at[donor].add(-moved).at[sink].add(moved)
    labels = jnp.searchsorted(jnp.cumsum(tallies), jnp.arange(rows * top), side="right").astype(jnp.int32)
    table = labels.reshape(top, rows).T
    table = table[jax.random.permutation(jax.random.fold_in(own, 1), rows)]
    offset_by = jax.random.randint(jax.random.fold_in(own, 2), (rows, 1), 0, top)
    return jnp.take_along_axis(table, (jnp.arange(top)[None, :] + offset_by) % top, axis=1)


def portions_of(count, total, bound, slope, full):
    portions = [(1 << 20) // math.isqrt(grade ** slope) + 1 for grade in range(1, count + 1)]
    largest = bound if full else min(bound, max(-(-total // count), total * portions[0] // sum(portions)))
    least = 1 if total - largest >= count - 1 else 0
    counts, rest = [largest] + [least] * (count - 1), total - largest - least * (count - 1)
    while rest > 0:
        candidates = [i for i in range(1, count) if counts[i] < largest] or [i for i in range(1, count) if counts[i] < bound]
        mass, left = sum([portions[i] for i in candidates]), rest
        for i in candidates:
            extra = min(bound - counts[i], max(1, left * portions[i] // mass), rest)
            counts[i] = counts[i] + extra
            rest = rest - extra
    return np.array(counts)


def centred(own_key, shape, spread, bound, shards=(), kind=jnp.bfloat16):
    factor_of = steps_of(own_key, shape, shards, -0.22, 0.18) if shards else 1.0
    entries = jax.random.normal(own_key, shape, jnp.float32) * spread * factor_of
    return jnp.minimum(jnp.maximum(entries, -bound), bound).astype(kind)


def setup_inputs(seed: int = 0) -> dict:
    streams_of = jax.random.split(jax.random.key(seed), 6)
    grad_out = centred(streams_of[0], (TOKENS, D), 1.0, 6.0, ((0, 16), (1, 2)))
    hidden_in = draw_hidden_in(jax.random.fold_in(streams_of[5], 71), 0)
    gate_prob = jnp.clip(jnp.exp(math.log(1.0) - 2.3025851 * jax.random.uniform(streams_of[2], (TOKENS,), jnp.float32) ** steps_of(streams_of[2], (TOKENS,), ((0, 16),), -0.2, 0.2)), 0.1, 1.0)
    expert_ids_keys = jax.random.split(jax.random.fold_in(streams_of[3], 1), TOKENS // TOK_DEV)
    expert_ids_turns = jax.random.permutation(jax.random.fold_in(streams_of[3], 3), TOKENS // TOK_DEV)
    expert_ids = jax.vmap(lambda own, number: assign_block(jax.random.fold_in(streams_of[3], 2), own, number, TOK_DEV, EXPERTS, 1, CAP, 2))(expert_ids_keys, expert_ids_turns).reshape((TOKENS, 1))
    w_down = centred(streams_of[4], (EXPERTS, FF, D), FF ** -0.5, 0.09375, ((0, 16), (1, 2)))
    return {"grad_out": grad_out, "hidden_in": hidden_in, "gate_prob": gate_prob, "expert_ids": expert_ids, "w_down": w_down}


def reference(grad_out, hidden_in, gate_prob, expert_ids, w_down):
    tokens = grad_out.shape[0]
    chosen = expert_ids[:, 0].astype(jnp.int32)
    onehot = (chosen[:, None] == jnp.arange(EXPERTS, dtype=jnp.int32)[None, :]).astype(jnp.int32)
    blocks = onehot.reshape(N_EXPERT, TOK_DEV, EXPERTS)
    earlier = jnp.sum((jnp.cumsum(blocks, axis=1) - 1) * blocks, axis=2).reshape(tokens).astype(jnp.int32)
    anchor = (jnp.arange(tokens, dtype=jnp.int32) // TOK_DEV).astype(jnp.int32)
    column = (anchor * CAP + earlier).astype(jnp.int32)
    table = jnp.full((EXPERTS, N_EXPERT * CAP), tokens, jnp.int32).at[chosen, column].set(jnp.arange(tokens, dtype=jnp.int32))
    padded = jnp.concatenate([grad_out, jnp.zeros((1, D), grad_out.dtype)], axis=0)

    def one_expert(pair):
        index, weight = pair
        return jnp.dot(padded[index], weight.T, preferred_element_type=jnp.float32).astype(jnp.bfloat16)

    rows = lax.map(one_expert, (table, w_down))
    returned = jnp.zeros((tokens + 1, FF), jnp.bfloat16).at[table.reshape(-1)].set(rows.reshape(-1, FF))
    returned = returned[:tokens].astype(jnp.float32)
    grad_hidden = (gate_prob[:, None] * returned).astype(jnp.bfloat16)
    grad_gate = jnp.sum(hidden_in.astype(jnp.float32) * returned, axis=1)
    return grad_hidden, grad_gate
```

```python
import functools

import jax
import jax.numpy as jnp
from jax import lax
from jax.experimental import pallas as pl
from jax.experimental.pallas import tpu as pltpu
from jax.sharding import PartitionSpec as P

MESH = pl.DeviceIdType.MESH
LANES = 128


def across(index, step, count):
    total, bit = 0, 1
    while bit < count:
        total = total + lax.rem(lax.div(index, bit) + lax.div(step, bit), 2) * bit
        bit *= 2
    return total


def steps_of(pair, groups):
    quarter = groups // 4
    near = jnp.where(pair < quarter, quarter + pair, lax.rem(pair + 1, quarter))
    return groups // 2 + pair, near


def tiled_lanes(column, width):
    return jnp.concatenate([column] * (width // LANES), axis=1)


def kernel(
    groups,
    parts,
    capacity,
    tile,
    grad_ref,
    hidden_ref,
    gate_ref,
    ids_ref,
    w_ref,
    out_ref,
    gate_out_ref,
    grad,
    hidden,
    weight,
    outgoing,
    arrived,
    product,
    returned,
    total,
    slot_row,
    slot_column,
    gate_column,
    sums,
    gate_sums,
    local_sem,
    send_sem,
    recv_sem,
    peer_send_sem,
    peer_recv_sem,
    back_send_sem,
    back_recv_sem,
    gate_send_sem,
    gate_recv_sem,
):
    me = lax.axis_index("expert")
    part = lax.axis_index("tensor")
    pairs = groups // 2
    both = 2 * capacity
    tokens, width = grad.shape
    units = weight.shape[0]

    load_grad = pltpu.make_async_copy(grad_ref, grad, local_sem.at[0])
    load_weight = pltpu.make_async_copy(w_ref, weight, local_sem.at[1])
    load_hidden = pltpu.make_async_copy(hidden_ref, hidden, local_sem.at[2])
    load_grad.start()
    load_weight.start()
    load_hidden.start()

    barrier = pltpu.get_barrier_semaphore()

    @pl.loop(1, groups)
    def _(step):
        pl.semaphore_signal(
            barrier, inc=1, device_id=(across(me, step, groups), part), device_id_type=MESH
        )

    for hop in range(1, parts):
        pl.semaphore_signal(
            barrier, inc=1, device_id=(me, lax.rem(part + hop, parts)), device_id_type=MESH
        )

    ids = ids_ref[...]
    ids_column = jnp.broadcast_to(ids, (LANES, tokens)).T
    earlier = jnp.zeros((1, tokens), jnp.int32)
    for start in range(0, tokens, LANES):
        rows = min(LANES, tokens - start)
        shape = (rows, tokens)
        same = tiled_lanes(ids_column[start : start + rows], tokens) == ids
        before = lax.broadcasted_iota(jnp.int32, shape, 0) + start < lax.broadcasted_iota(
            jnp.int32, shape, 1
        )
        earlier = earlier + jnp.sum(
            jnp.where(same & before, 1, 0), axis=0, keepdims=True
        )
    slots = ids * capacity + earlier
    slot_row[...] = slots
    slot_column[...] = jnp.broadcast_to(slots, (LANES, tokens)).T
    gate_column[...] = jnp.broadcast_to(gate_ref[...], (LANES, tokens)).T

    load_grad.wait()

    def rows_of(pair):
        return pl.ds(pl.multiple_of(pair * both, both), both)

    def rows_at(slot):
        return pl.ds(pl.multiple_of(slot * capacity, capacity), capacity)

    def pack(pair, target):
        far, near = steps_of(pair, groups)
        row = lax.broadcasted_iota(jnp.int32, (capacity, tokens), 0)
        chosen = [
            jnp.where(slot_row[...] == row + across(me, step, groups) * capacity, 1.0, 0.0)
            for step in (far, near)
        ]
        pick = jnp.concatenate(chosen, axis=0).astype(jnp.bfloat16)
        rows = jnp.dot(pick, grad[...], preferred_element_type=jnp.float32)
        target[rows_of(pair), :] = rows.astype(jnp.bfloat16)

    def outward(slot, step):
        return pltpu.make_async_remote_copy(
            src_ref=outgoing.at[rows_at(slot)],
            dst_ref=arrived.at[part, rows_at(slot)],
            send_sem=send_sem.at[slot],
            recv_sem=recv_sem.at[slot],
            device_id=(across(me, step, groups), part),
            device_id_type=MESH,
        )

    def sideways(pair, hop):
        return pltpu.make_async_remote_copy(
            src_ref=arrived.at[part, rows_of(pair)],
            dst_ref=arrived.at[part, rows_of(pair)],
            send_sem=peer_send_sem.at[hop - 1, pair],
            recv_sem=peer_recv_sem.at[hop - 1, pair],
            device_id=(me, lax.rem(part + hop, parts)),
            device_id_type=MESH,
        )

    def sideways_in(pair, hop):
        sender = lax.rem(part + parts - hop, parts)
        return pltpu.make_async_remote_copy(
            src_ref=arrived.at[sender, rows_of(pair)],
            dst_ref=arrived.at[sender, rows_of(pair)],
            send_sem=peer_send_sem.at[hop - 1, pair],
            recv_sem=peer_recv_sem.at[hop - 1, pair],
            device_id=(me, lax.rem(part + hop, parts)),
            device_id_type=MESH,
        )

    def homeward(slot, step):
        return pltpu.make_async_remote_copy(
            src_ref=product.at[rows_at(slot)],
            dst_ref=returned.at[rows_at(slot)],
            send_sem=back_send_sem.at[slot],
            recv_sem=back_recv_sem.at[slot],
            device_id=(across(me, step, groups), part),
            device_id_type=MESH,
        )

    own = pairs - 1
    own_rows = pl.ds((groups - 1) * capacity, capacity)

    pack(0, outgoing)
    pl.semaphore_wait(barrier, groups - 1 + parts - 1)
    outward(0, groups // 2).start()
    outward(1, steps_of(0, groups)[1]).start()

    @pl.loop(1, pairs)
    def _(pair):
        pack(pair, outgoing)
        far, near = steps_of(pair, groups)
        outward(2 * pair, far).start()

        @pl.when(pair < own)
        def _():
            outward(2 * pair + 1, near).start()

    arrived[part, own_rows, :] = outgoing[own_rows, :]

    def multiply(pair):
        @pl.loop(0, units // tile)
        def _(block):
            columns = pl.ds(pl.multiple_of(block * tile, tile), tile)
            value = jnp.zeros((both, tile), jnp.float32)
            for piece in range(parts):
                value = value + lax.dot_general(
                    arrived[piece, rows_of(pair), :],
                    weight[columns, piece * width : (piece + 1) * width],
                    (((1,), (1,)), ((), ())),
                    preferred_element_type=jnp.float32,
                )
            product[rows_of(pair), columns] = value.astype(jnp.bfloat16)

    @pl.loop(0, pairs + 1)
    def _(turn):
        @pl.when(turn < pairs)
        def _():
            far, near = steps_of(turn, groups)
            outward(2 * turn, far).wait_recv()

            @pl.when(turn < own)
            def _():
                outward(2 * turn + 1, near).wait_recv()

            for hop in range(1, parts):
                sideways(turn, hop).start()

        @pl.when(turn == 0)
        def _():
            load_weight.wait()

        @pl.when(turn > 0)
        def _():
            pair = turn - 1
            for hop in range(1, parts):
                sideways_in(pair, hop).wait_recv()
            multiply(pair)
            far, near = steps_of(pair, groups)
            homeward(2 * pair, far).start()

            @pl.when(pair < own)
            def _():
                homeward(2 * pair + 1, near).start()

    returned[own_rows, :] = product[own_rows, :]
    load_hidden.wait()
    total[...] = jnp.zeros_like(total)
    sums[...] = jnp.zeros_like(sums)

    def placement(pair, rows):
        far, near = steps_of(pair, groups)
        lane = lax.broadcasted_iota(jnp.int32, (1, both), 1)
        wanted = jnp.where(
            lane < capacity,
            lane + across(me, far, groups) * capacity,
            lane + (across(me, near, groups) - 1) * capacity,
        )
        hit = slot_column[rows, :both] == wanted
        return jnp.where(hit, 1.0, 0.0).astype(jnp.bfloat16)

    def wait_home(pair):
        far, near = steps_of(pair, groups)
        homeward(2 * pair, far).wait_recv()

        @pl.when(pair < own)
        def _():
            homeward(2 * pair + 1, near).wait_recv()

    everything = pl.ds(0, tokens)

    @pl.loop(0, own)
    def _(pair):
        wait_home(pair)
        place = placement(pair, everything)

        @pl.loop(0, units // tile)
        def _(block):
            columns = pl.ds(pl.multiple_of(block * tile, tile), tile)
            total[:, columns] += jnp.dot(
                place, returned[rows_of(pair), columns], preferred_element_type=jnp.float32
            )

    wait_home(own)
    chunk = min(LANES, tokens)

    @pl.loop(0, tokens // chunk)
    def _(part_of):
        rows = pl.ds(pl.multiple_of(part_of * chunk, chunk), chunk)
        place = placement(own, rows)
        gate = tiled_lanes(gate_column[rows, :], tile)

        @pl.loop(0, units // tile)
        def _(block):
            columns = pl.ds(pl.multiple_of(block * tile, tile), tile)
            back = total[rows, columns] + jnp.dot(
                place, returned[rows_of(own), columns], preferred_element_type=jnp.float32
            )
            out_ref[rows, columns] = (gate * back).astype(jnp.bfloat16)
            terms = hidden[rows, columns].astype(jnp.float32) * back
            sums[rows, :] += sum(
                terms[:, at : at + LANES] for at in range(0, tile, LANES)
            )

    row = jnp.sum(sums[...].T, axis=0, keepdims=True)
    gate_sums[part] = jnp.broadcast_to(row, (8, tokens))

    def gate_copy(hop, sender):
        return pltpu.make_async_remote_copy(
            src_ref=gate_sums.at[sender],
            dst_ref=gate_sums.at[sender],
            send_sem=gate_send_sem.at[hop - 1],
            recv_sem=gate_recv_sem.at[hop - 1],
            device_id=(me, lax.rem(part + hop, parts)),
            device_id_type=MESH,
        )

    for hop in range(1, parts):
        gate_copy(hop, part).start()

    @pl.loop(0, pairs)
    def _(pair):
        far, near = steps_of(pair, groups)
        outward(2 * pair, far).wait_send()
        homeward(2 * pair, far).wait_send()
        for hop in range(1, parts):
            sideways(pair, hop).wait_send()

        @pl.when(pair < own)
        def _():
            outward(2 * pair + 1, near).wait_send()
            homeward(2 * pair + 1, near).wait_send()

    for hop in range(1, parts):
        gate_copy(hop, part).wait_send()
        gate_copy(hop, lax.rem(part + parts - hop, parts)).wait_recv()
    result = gate_sums[0]
    for piece in range(1, parts):
        result = result + gate_sums[piece]
    gate_out_ref[...] = result[:1]


def body(groups, parts, grad_out, hidden_in, gate_prob, expert_ids, w_down):
    tokens, width = grad_out.shape
    _, units, features = w_down.shape
    capacity = 2 * tokens // (groups * w_down.shape[0])
    tile = min(512, units)
    rows = groups * capacity
    dma = pltpu.SemaphoreType.DMA
    hops = max(parts - 1, 1)
    grad_hidden, grad_gate = pl.pallas_call(
        functools.partial(kernel, groups, parts, capacity, tile),
        out_shape=(
            jax.ShapeDtypeStruct((tokens, units), jnp.bfloat16),
            jax.ShapeDtypeStruct((1, tokens), jnp.float32),
        ),
        in_specs=[
            pl.BlockSpec(memory_space=pl.ANY),
            pl.BlockSpec(memory_space=pl.ANY),
            pl.BlockSpec(memory_space=pltpu.VMEM),
            pl.BlockSpec(memory_space=pltpu.VMEM),
            pl.BlockSpec(memory_space=pl.ANY),
        ],
        out_specs=(
            pl.BlockSpec(memory_space=pltpu.VMEM),
            pl.BlockSpec(memory_space=pltpu.VMEM),
        ),
        scratch_shapes=[
            pltpu.VMEM((tokens, width), jnp.bfloat16),
            pltpu.VMEM((tokens, units), jnp.bfloat16),
            pltpu.VMEM((units, features), jnp.bfloat16),
            pltpu.VMEM((rows, width), jnp.bfloat16),
            pltpu.VMEM((parts, rows, width), jnp.bfloat16),
            pltpu.VMEM((rows, units), jnp.bfloat16),
            pltpu.VMEM((rows, units), jnp.bfloat16),
            pltpu.VMEM((tokens, units), jnp.float32),
            pltpu.VMEM((1, tokens), jnp.int32),
            pltpu.VMEM((tokens, LANES), jnp.int32),
            pltpu.VMEM((tokens, LANES), jnp.float32),
            pltpu.VMEM((tokens, LANES), jnp.float32),
            pltpu.VMEM((parts, 8, tokens), jnp.float32),
            dma((3,)),
            dma((groups,)),
            dma((groups,)),
            dma((hops, groups // 2)),
            dma((hops, groups // 2)),
            dma((groups,)),
            dma((groups,)),
            dma((hops,)),
            dma((hops,)),
        ],
        compiler_params=pltpu.CompilerParams(
            collective_id=0, has_side_effects=True, vmem_limit_bytes=56 * 1024 * 1024
        ),
    )(
        grad_out,
        hidden_in,
        gate_prob.reshape(1, tokens),
        expert_ids.reshape(1, tokens),
        w_down.reshape(units, features),
    )
    return grad_hidden, grad_gate.reshape(tokens)


def solution(mesh):
    return jax.shard_map(
        functools.partial(body, mesh.shape["expert"], mesh.shape["tensor"]),
        mesh=mesh,
        in_specs=(
            P("expert", "tensor"),
            P("expert", "tensor"),
            P("expert"),
            P("expert", None),
            P("expert", "tensor", None),
        ),
        out_specs=(P("expert", "tensor"), P("expert")),
        check_vma=False,
    )
```

```python
import functools

import jax
import jax.numpy as jnp
from jax import lax
from jax.experimental import pallas as pl
from jax.experimental.pallas import tpu as pltpu
from jax.sharding import PartitionSpec as P

MESH = pl.DeviceIdType.MESH
LANES = 128
FAR = "far"


def across(index, step, count):
    total, bit = 0, 1
    while bit < count:
        total = total + lax.rem(lax.div(index, bit) + lax.div(step, bit), 2) * bit
        bit *= 2
    return total


def steps_of(pair, groups):
    quarter = groups // 4
    near = jnp.where(pair < quarter, quarter + pair, lax.rem(pair + 1, quarter))
    return groups // 2 + pair, near


def tiled_lanes(column, width):
    return jnp.concatenate([column] * (width // LANES), axis=1)


def kernel(
    groups,
    parts,
    capacity,
    tile,
    spill,
    grad_ref,
    hidden_ref,
    ids_ref,
    w_ref,
    out_ref,
    gate_out_ref,
    most_ref,
    grad,
    hidden,
    weight,
    outgoing,
    arrived,
    product,
    returned,
    total,
    slot_row,
    slot_column,
    sums,
    gate_sums,
    local_sem,
    send_sem,
    recv_sem,
    peer_send_sem,
    peer_recv_sem,
    back_send_sem,
    back_recv_sem,
    gate_send_sem,
    gate_recv_sem,
    *spill_refs,
):
    me = lax.axis_index("expert")
    part = lax.axis_index("tensor")
    pairs = groups // 2
    both = 2 * capacity
    tokens, width = grad.shape
    units = weight.shape[0]
    middle = groups // 2
    half = capacity // 2
    side = lax.div(me, middle)
    local = me - side * middle
    if spill:
        (
            spill_column,
            place_out,
            place_in,
            counts,
            spill_out,
            spill_in,
            relay_out,
            relay_back,
            spill_back,
            spill_home,
            place_sem,
            count_send_sem,
            count_recv_sem,
            spill_sem,
            relay_send_sem,
            relay_recv_sem,
            relay_back_send_sem,
            relay_back_recv_sem,
            spill_back_sem,
        ) = spill_refs
        lanes = place_in.shape[1]
    far_rows = half if spill else capacity

    load_grad = pltpu.make_async_copy(grad_ref, grad, local_sem.at[0])
    load_weight = pltpu.make_async_copy(w_ref, weight, local_sem.at[1])
    load_hidden = pltpu.make_async_copy(hidden_ref, hidden, local_sem.at[2])
    load_grad.start()
    load_weight.start()
    load_hidden.start()

    barrier = pltpu.get_barrier_semaphore()

    @pl.loop(1, groups)
    def _(step):
        pl.semaphore_signal(
            barrier, inc=1, device_id=(across(me, step, groups), part), device_id_type=MESH
        )

    for hop in range(1, parts):
        pl.semaphore_signal(
            barrier, inc=1, device_id=(me, lax.rem(part + hop, parts)), device_id_type=MESH
        )

    ids = ids_ref[...]
    ids_column = jnp.broadcast_to(ids, (LANES, tokens)).T
    earlier = jnp.zeros((1, tokens), jnp.int32)
    for start in range(0, tokens, LANES):
        rows = min(LANES, tokens - start)
        shape = (rows, tokens)
        same = tiled_lanes(ids_column[start : start + rows], tokens) == ids
        before = lax.broadcasted_iota(jnp.int32, shape, 0) + start < lax.broadcasted_iota(
            jnp.int32, shape, 1
        )
        earlier = earlier + jnp.sum(
            jnp.where(same & before, 1, 0), axis=0, keepdims=True
        )
    slots = ids * capacity + earlier
    slot_row[...] = slots
    slot_column[...] = jnp.broadcast_to(slots, (LANES, tokens)).T
    if spill:
        expert_side = jnp.where(ids >= middle, 1, 0)
        over = jnp.where((expert_side != side) & (earlier >= half), 1, 0)
        over_column = jnp.broadcast_to(over, (LANES, tokens)).T
        order = jnp.zeros((1, tokens), jnp.int32)
        for start in range(0, tokens, LANES):
            rows = min(LANES, tokens - start)
            shape = (rows, tokens)
            before = lax.broadcasted_iota(jnp.int32, shape, 0) + start < lax.broadcasted_iota(
                jnp.int32, shape, 1
            )
            ahead = tiled_lanes(over_column[start : start + rows], tokens)
            order = order + jnp.sum(jnp.where(before, ahead, 0), axis=0, keepdims=True)
        order = jnp.where(over > 0, order, -1)
        spill_column[...] = jnp.broadcast_to(order, (LANES, tokens)).T
        spot = (ids - expert_side * middle) * half + earlier - half + 1
        spot_column = jnp.broadcast_to(spot, (LANES, tokens)).T
        match = tiled_lanes(spill_column[...], lanes) == lax.broadcasted_iota(
            jnp.int32, (tokens, lanes), 1
        )
        place_out[...] = (
            jnp.sum(
                jnp.where(match, tiled_lanes(spot_column, lanes), 0), axis=0, keepdims=True
            )
            - 1
        )
        counts[0] = jnp.broadcast_to(jnp.sum(over, axis=1, keepdims=True), (1, LANES))
        spill_in[spill:, :] = jnp.zeros((lanes - spill, width), jnp.bfloat16)
        spill_home[spill:, :] = jnp.zeros((lanes - spill, units), jnp.bfloat16)

        @pl.loop(0, pairs)
        def _(pair):
            unused = pl.ds(pl.multiple_of(pair * both + half, half), half)
            returned[unused, :] = jnp.zeros((half, units), jnp.bfloat16)


    load_grad.wait()

    def rows_of(pair):
        return pl.ds(pl.multiple_of(pair * both, both), both)

    def pack(pair, target):
        far, near = steps_of(pair, groups)
        row = lax.broadcasted_iota(jnp.int32, (capacity, tokens), 0)
        chosen = [
            jnp.where(slot_row[...] == row + across(me, step, groups) * capacity, 1.0, 0.0)
            for step in (far, near)
        ]
        pick = jnp.concatenate(chosen, axis=0).astype(jnp.bfloat16)
        rows = jnp.dot(pick, grad[...], preferred_element_type=jnp.float32)
        target[rows_of(pair), :] = rows.astype(jnp.bfloat16)

    def sent_rows(slot, step):
        size = far_rows if step is FAR else capacity
        return pl.ds(pl.multiple_of(slot * capacity, capacity), size)

    def outward(slot, step, kind=None):
        return pltpu.make_async_remote_copy(
            src_ref=outgoing.at[sent_rows(slot, kind)],
            dst_ref=arrived.at[part, sent_rows(slot, kind)],
            send_sem=send_sem.at[slot],
            recv_sem=recv_sem.at[slot],
            device_id=(across(me, step, groups), part),
            device_id_type=MESH,
        )

    def sideways(pair, hop):
        return pltpu.make_async_remote_copy(
            src_ref=arrived.at[part, rows_of(pair)],
            dst_ref=arrived.at[part, rows_of(pair)],
            send_sem=peer_send_sem.at[hop - 1, pair],
            recv_sem=peer_recv_sem.at[hop - 1, pair],
            device_id=(me, lax.rem(part + hop, parts)),
            device_id_type=MESH,
        )

    def sideways_in(pair, hop):
        sender = lax.rem(part + parts - hop, parts)
        return pltpu.make_async_remote_copy(
            src_ref=arrived.at[sender, rows_of(pair)],
            dst_ref=arrived.at[sender, rows_of(pair)],
            send_sem=peer_send_sem.at[hop - 1, pair],
            recv_sem=peer_recv_sem.at[hop - 1, pair],
            device_id=(me, lax.rem(part + hop, parts)),
            device_id_type=MESH,
        )

    def homeward(slot, step, kind=None):
        return pltpu.make_async_remote_copy(
            src_ref=product.at[sent_rows(slot, kind)],
            dst_ref=returned.at[sent_rows(slot, kind)],
            send_sem=back_send_sem.at[slot],
            recv_sem=back_recv_sem.at[slot],
            device_id=(across(me, step, groups), part),
            device_id_type=MESH,
        )

    own = pairs - 1
    own_rows = pl.ds((groups - 1) * capacity, capacity)

    def send_pair(pair):
        far, near = steps_of(pair, groups)
        outward(2 * pair, far, FAR).start()

        @pl.when(pair < own)
        def _():
            outward(2 * pair + 1, near).start()

    if spill:
        mirror = (across(me, middle, groups), part)

        def to_mirror(source, target, sems):
            return pltpu.make_async_remote_copy(
                src_ref=source,
                dst_ref=target,
                send_sem=sems.at[0],
                recv_sem=sems.at[1],
                device_id=mirror,
                device_id_type=MESH,
            )

        def send_count(step):
            return pltpu.make_async_remote_copy(
                src_ref=counts.at[0],
                dst_ref=counts.at[step],
                send_sem=count_send_sem.at[step],
                recv_sem=count_recv_sem.at[step],
                device_id=(across(me, step, groups), part),
                device_id_type=MESH,
            )

        def half_rows(index):
            return pl.ds(pl.multiple_of(index * half, half), half)

        def second_half(pair):
            return pl.ds(pl.multiple_of(pair * both + half, half), half)

        def relay(step):
            target = across(me, step, groups)
            return pltpu.make_async_remote_copy(
                src_ref=relay_out.at[half_rows(target - side * middle)],
                dst_ref=arrived.at[part, second_half(step)],
                send_sem=relay_send_sem.at[step],
                recv_sem=relay_recv_sem.at[step],
                device_id=(target, part),
                device_id_type=MESH,
            )

        def relay_home(step):
            return pltpu.make_async_remote_copy(
                src_ref=product.at[second_half(step)],
                dst_ref=relay_back.at[half_rows(local)],
                send_sem=relay_back_send_sem.at[step],
                recv_sem=relay_back_recv_sem.at[step],
                device_id=(across(me, step, groups), part),
                device_id_type=MESH,
            )

        def relay_home_in(step):
            sender = across(me, step, groups) - side * middle
            return pltpu.make_async_remote_copy(
                src_ref=product.at[second_half(step)],
                dst_ref=relay_back.at[half_rows(sender)],
                send_sem=relay_back_send_sem.at[step],
                recv_sem=relay_back_recv_sem.at[step],
                device_id=(across(me, step, groups), part),
                device_id_type=MESH,
            )

        place_copy = to_mirror(place_out, place_in, place_sem)
        spill_copy = to_mirror(spill_out, spill_in.at[pl.ds(0, spill)], spill_sem)
        spill_back_copy = to_mirror(
            spill_back, spill_home.at[pl.ds(0, spill)], spill_back_sem
        )
        index = lax.broadcasted_iota(jnp.int32, (spill, tokens), 0)
        pick = jnp.where(order == index, 1.0, 0.0).astype(jnp.bfloat16)
        spill_out[...] = jnp.dot(
            pick, grad[...], preferred_element_type=jnp.float32
        ).astype(jnp.bfloat16)
        pl.semaphore_wait(barrier, groups - 1 + parts - 1)
        place_copy.start()
        spill_copy.start()
        early = pairs // 2

        @pl.loop(0, early)
        def _(pair):
            pack(pair, outgoing)
            send_pair(pair)

        place_copy.wait_recv()
        spill_copy.wait_recv()
        index = lax.broadcasted_iota(jnp.int32, (middle * half, lanes), 0)
        pick = jnp.where(place_in[...] == index, 1.0, 0.0).astype(jnp.bfloat16)
        relay_out[...] = jnp.dot(
            pick, spill_in[...], preferred_element_type=jnp.float32
        ).astype(jnp.bfloat16)

        @pl.loop(1, middle)
        def _(step):
            relay(step).start()

        arrived[part, half:capacity, :] = relay_out[half_rows(local), :]

        @pl.loop(early, pairs)
        def _(pair):
            pack(pair, outgoing)
            send_pair(pair)

        @pl.loop(1, groups)
        def _(step):
            send_count(step).start()

    else:
        pack(0, outgoing)
        pl.semaphore_wait(barrier, groups - 1 + parts - 1)
        send_pair(0)

        @pl.loop(1, pairs)
        def _(pair):
            pack(pair, outgoing)
            send_pair(pair)

    arrived[part, own_rows, :] = outgoing[own_rows, :]

    def multiply(pair):
        @pl.loop(0, units // tile)
        def _(block):
            columns = pl.ds(pl.multiple_of(block * tile, tile), tile)
            value = jnp.zeros((both, tile), jnp.float32)
            for piece in range(parts):
                value = value + lax.dot_general(
                    arrived[piece, rows_of(pair), :],
                    weight[columns, piece * width : (piece + 1) * width],
                    (((1,), (1,)), ((), ())),
                    preferred_element_type=jnp.float32,
                )
            product[rows_of(pair), columns] = value.astype(jnp.bfloat16)

    @pl.loop(0, pairs + 1)
    def _(turn):
        @pl.when(turn < pairs)
        def _():
            far, near = steps_of(turn, groups)
            outward(2 * turn, far, FAR).wait_recv()

            @pl.when(turn < own)
            def _():
                outward(2 * turn + 1, near).wait_recv()

            if spill:

                @pl.when(turn > 0)
                def _():
                    relay(turn).wait_recv()

            for hop in range(1, parts):
                sideways(turn, hop).start()

        @pl.when(turn == 0)
        def _():
            load_weight.wait()

        @pl.when(turn > 0)
        def _():
            pair = turn - 1
            for hop in range(1, parts):
                sideways_in(pair, hop).wait_recv()
            multiply(pair)
            far, near = steps_of(pair, groups)
            if spill:

                @pl.when(pair > 0)
                def _():
                    relay_home(pair).start()

            homeward(2 * pair, far, FAR).start()

            @pl.when(pair < own)
            def _():
                homeward(2 * pair + 1, near).start()

    if spill:
        relay_back[half_rows(local), :] = product[half:capacity, :]

        @pl.loop(1, middle)
        def _(step):
            relay_home_in(step).wait_recv()

        column = jnp.broadcast_to(place_in[...], (LANES, lanes)).T[:spill]
        index = lax.broadcasted_iota(jnp.int32, (spill, middle * half), 1)
        wide = jnp.concatenate([column] * -(-middle * half // LANES), axis=1)
        pick = jnp.where(wide[:, : middle * half] == index, 1.0, 0.0).astype(jnp.bfloat16)

        @pl.loop(0, units // tile)
        def _(block):
            columns = pl.ds(pl.multiple_of(block * tile, tile), tile)
            spill_back[:, columns] = jnp.dot(
                pick, relay_back[:, columns], preferred_element_type=jnp.float32
            ).astype(jnp.bfloat16)

        spill_back_copy.start()

    returned[own_rows, :] = product[own_rows, :]
    load_hidden.wait()
    total[...] = jnp.zeros_like(total)
    sums[...] = jnp.zeros_like(sums)

    def placement(pair, rows):
        far, near = steps_of(pair, groups)
        lane = lax.broadcasted_iota(jnp.int32, (1, both), 1)
        wanted = jnp.where(
            lane < capacity,
            lane + across(me, far, groups) * capacity,
            lane + (across(me, near, groups) - 1) * capacity,
        )
        if spill:
            wanted = jnp.where((lane >= half) & (lane < capacity), -1, wanted)
        hit = slot_column[rows, :both] == wanted
        return jnp.where(hit, 1.0, 0.0).astype(jnp.bfloat16)

    def wait_home(pair):
        far, near = steps_of(pair, groups)
        homeward(2 * pair, far, FAR).wait_recv()

        @pl.when(pair < own)
        def _():
            homeward(2 * pair + 1, near).wait_recv()

    everything = pl.ds(0, tokens)

    @pl.loop(0, pairs if spill else own)
    def _(pair):
        wait_home(pair)
        place = placement(pair, everything)

        @pl.loop(0, units // tile)
        def _(block):
            columns = pl.ds(pl.multiple_of(block * tile, tile), tile)
            total[:, columns] += jnp.dot(
                place, returned[rows_of(pair), columns], preferred_element_type=jnp.float32
            )

    if spill:
        spill_back_copy.wait_recv()
    else:
        wait_home(own)
    chunk = min(LANES, tokens)

    @pl.loop(0, tokens // chunk)
    def _(part_of):
        rows = pl.ds(pl.multiple_of(part_of * chunk, chunk), chunk)
        if spill:
            lane = lax.broadcasted_iota(jnp.int32, (chunk, lanes), 1)
            hit = tiled_lanes(spill_column[rows, :], lanes) == lane
            place = jnp.where(hit, 1.0, 0.0).astype(jnp.bfloat16)
        else:
            place = placement(own, rows)

        @pl.loop(0, units // tile)
        def _(block):
            columns = pl.ds(pl.multiple_of(block * tile, tile), tile)
            last = spill_home[:, columns] if spill else returned[rows_of(own), columns]
            back = total[rows, columns] + jnp.dot(
                place, last, preferred_element_type=jnp.float32
            )
            out_ref[rows, columns] = back.astype(jnp.bfloat16)
            terms = hidden[rows, columns].astype(jnp.float32) * back
            sums[rows, :] += sum(
                terms[:, at : at + LANES] for at in range(0, tile, LANES)
            )

    row = jnp.sum(sums[...].T, axis=0, keepdims=True)
    gate_sums[part] = jnp.broadcast_to(row, (8, tokens))

    def gate_copy(hop, sender):
        return pltpu.make_async_remote_copy(
            src_ref=gate_sums.at[sender],
            dst_ref=gate_sums.at[sender],
            send_sem=gate_send_sem.at[hop - 1],
            recv_sem=gate_recv_sem.at[hop - 1],
            device_id=(me, lax.rem(part + hop, parts)),
            device_id_type=MESH,
        )

    for hop in range(1, parts):
        gate_copy(hop, part).start()

    @pl.loop(0, pairs)
    def _(pair):
        far, near = steps_of(pair, groups)
        outward(2 * pair, far, FAR).wait_send()
        homeward(2 * pair, far, FAR).wait_send()
        for hop in range(1, parts):
            sideways(pair, hop).wait_send()

        @pl.when(pair < own)
        def _():
            outward(2 * pair + 1, near).wait_send()
            homeward(2 * pair + 1, near).wait_send()

    if spill:
        place_copy.wait_send()
        spill_copy.wait_send()
        spill_back_copy.wait_send()

        @pl.loop(1, middle)
        def _(step):
            relay(step).wait_send()
            relay_home(step).wait_send()

        @pl.loop(1, groups)
        def _(step):
            send_count(step).wait()

        most_ref[...] = jnp.max(counts[...], axis=0)
    else:
        most_ref[...] = jnp.zeros_like(most_ref)
    for hop in range(1, parts):
        gate_copy(hop, part).wait_send()
        gate_copy(hop, lax.rem(part + parts - hop, parts)).wait_recv()
    result = gate_sums[0]
    for piece in range(1, parts):
        result = result + gate_sums[piece]
    gate_out_ref[...] = result[:1]


def call(groups, parts, capacity, spill, grad_out, hidden_in, ids, w_down):
    tokens, width = grad_out.shape
    units, features = w_down.shape
    tile = min(512, units)
    rows = groups * capacity
    dma = pltpu.SemaphoreType.DMA
    hops = max(parts - 1, 1)
    middle = groups // 2
    lanes = -(-spill // LANES) * LANES
    relayed = middle * capacity // 2
    spill_scratch = [
        pltpu.VMEM((tokens, LANES), jnp.int32),
        pltpu.VMEM((1, lanes), jnp.int32),
        pltpu.VMEM((1, lanes), jnp.int32),
        pltpu.VMEM((groups, 1, LANES), jnp.int32),
        pltpu.VMEM((spill, width), jnp.bfloat16),
        pltpu.VMEM((lanes, width), jnp.bfloat16),
        pltpu.VMEM((relayed, width), jnp.bfloat16),
        pltpu.VMEM((relayed, units), jnp.bfloat16),
        pltpu.VMEM((spill, units), jnp.bfloat16),
        pltpu.VMEM((lanes, units), jnp.bfloat16),
        dma((2,)),
        dma((groups,)),
        dma((groups,)),
        dma((2,)),
        dma((middle,)),
        dma((middle,)),
        dma((middle,)),
        dma((middle,)),
        dma((2,)),
    ]
    return pl.pallas_call(
        functools.partial(kernel, groups, parts, capacity, tile, spill),
        out_shape=(
            jax.ShapeDtypeStruct((tokens, units), jnp.bfloat16),
            jax.ShapeDtypeStruct((1, tokens), jnp.float32),
            jax.ShapeDtypeStruct((1, LANES), jnp.int32),
        ),
        in_specs=[
            pl.BlockSpec(memory_space=pl.ANY),
            pl.BlockSpec(memory_space=pl.ANY),
            pl.BlockSpec(memory_space=pltpu.VMEM),
            pl.BlockSpec(memory_space=pl.ANY),
        ],
        out_specs=(pl.BlockSpec(memory_space=pltpu.VMEM),) * 3,
        scratch_shapes=[
            pltpu.VMEM((tokens, width), jnp.bfloat16),
            pltpu.VMEM((tokens, units), jnp.bfloat16),
            pltpu.VMEM((units, features), jnp.bfloat16),
            pltpu.VMEM((rows, width), jnp.bfloat16),
            pltpu.VMEM((parts, rows, width), jnp.bfloat16),
            pltpu.VMEM((rows, units), jnp.bfloat16),
            pltpu.VMEM((rows, units), jnp.bfloat16),
            pltpu.VMEM((tokens, units), jnp.float32),
            pltpu.VMEM((1, tokens), jnp.int32),
            pltpu.VMEM((tokens, LANES), jnp.int32),
            pltpu.VMEM((tokens, LANES), jnp.float32),
            pltpu.VMEM((parts, 8, tokens), jnp.float32),
            dma((3,)),
            dma((groups,)),
            dma((groups,)),
            dma((hops, groups // 2)),
            dma((hops, groups // 2)),
            dma((groups,)),
            dma((groups,)),
            dma((hops,)),
            dma((hops,)),
        ]
        + (spill_scratch if spill else []),
        compiler_params=pltpu.CompilerParams(
            collective_id=1 if spill else 0,
            has_side_effects=True,
            vmem_limit_bytes=56 * 1024 * 1024,
        ),
    )(grad_out, hidden_in, ids, w_down)


def body(groups, parts, grad_out, hidden_in, gate_prob, expert_ids, w_down):
    tokens = grad_out.shape[0]
    experts, units, features = w_down.shape
    capacity = 2 * tokens // (groups * experts)
    args = (grad_out, hidden_in, expert_ids.reshape(1, tokens), w_down.reshape(units, features))
    whole = functools.partial(call, groups, parts, capacity, 0)
    spill = 9 * groups * capacity // 64 // 16 * 16
    if capacity % 32 == 0:
        back, gate_sum, most = call(groups, parts, capacity, spill, *args)
        back, gate_sum = lax.cond(
            most[0, 0] > spill,
            lambda back, gate_sum: whole(*args)[:2],
            lambda back, gate_sum: (back, gate_sum),
            back,
            gate_sum,
        )
    else:
        back, gate_sum, _ = whole(*args)
    grad_hidden = (gate_prob[:, None] * back.astype(jnp.float32)).astype(jnp.bfloat16)
    return grad_hidden, gate_sum.reshape(tokens)


def solution(mesh):
    return jax.shard_map(
        functools.partial(body, mesh.shape["expert"], mesh.shape["tensor"]),
        mesh=mesh,
        in_specs=(
            P("expert", "tensor"),
            P("expert", "tensor"),
            P("expert"),
            P("expert", None),
            P("expert", "tensor", None),
        ),
        out_specs=(P("expert", "tensor"), P("expert")),
        check_vma=False,
    )
```

```python
import functools

import jax
import jax.numpy as jnp
from jax import lax
from jax.experimental import pallas as pl
from jax.experimental.pallas import tpu as pltpu
from jax.sharding import PartitionSpec as P

MESH = pl.DeviceIdType.MESH
LANES = 128
FAR = "far"


def across(index, step, count):
    total, bit = 0, 1
    while bit < count:
        total = total + lax.rem(lax.div(index, bit) + lax.div(step, bit), 2) * bit
        bit *= 2
    return total


def steps_of(pair, groups):
    quarter = groups // 4
    near = jnp.where(pair < quarter, quarter + pair, lax.rem(pair + 1, quarter))
    return groups // 2 + pair, near


def tiled_lanes(column, width):
    return jnp.concatenate([column] * (width // LANES), axis=1)


def kernel(
    groups,
    parts,
    capacity,
    tile,
    spill,
    grad_ref,
    hidden_ref,
    ids_ref,
    w_ref,
    out_ref,
    gate_out_ref,
    most_ref,
    grad,
    hidden,
    weight,
    outgoing,
    arrived,
    product,
    returned,
    total,
    slot_row,
    slot_column,
    sums,
    gate_sums,
    local_sem,
    send_sem,
    recv_sem,
    peer_send_sem,
    peer_recv_sem,
    back_send_sem,
    back_recv_sem,
    gate_send_sem,
    gate_recv_sem,
    *spill_refs,
):
    me = lax.axis_index("expert")
    part = lax.axis_index("tensor")
    pairs = groups // 2
    tokens, width = grad.shape
    units = weight.shape[0]
    middle = groups // 2
    half = capacity // 2
    side = lax.div(me, middle)
    local = me - side * middle
    if spill:
        (
            spill_column,
            place_out,
            place_in,
            counts,
            spill_out,
            spill_in,
            relay_out,
            relay_back,
            spill_back,
            spill_home,
            place_sem,
            count_send_sem,
            count_recv_sem,
            spill_sem,
            relay_send_sem,
            relay_recv_sem,
            relay_back_send_sem,
            relay_back_recv_sem,
            spill_back_sem,
        ) = spill_refs
        lanes = place_in.shape[1]
    far_rows = half if spill else capacity
    both = far_rows + capacity
    relayed = middle * half

    load_grad = pltpu.make_async_copy(grad_ref, grad, local_sem.at[0])
    load_weight = pltpu.make_async_copy(w_ref, weight, local_sem.at[1])
    load_hidden = pltpu.make_async_copy(hidden_ref, hidden, local_sem.at[2])
    load_grad.start()
    load_weight.start()
    load_hidden.start()

    barrier = pltpu.get_barrier_semaphore()

    @pl.loop(1, groups)
    def _(step):
        pl.semaphore_signal(
            barrier, inc=1, device_id=(across(me, step, groups), part), device_id_type=MESH
        )

    for hop in range(1, parts):
        pl.semaphore_signal(
            barrier, inc=1, device_id=(me, lax.rem(part + hop, parts)), device_id_type=MESH
        )

    ids = ids_ref[...]
    ids_column = jnp.broadcast_to(ids, (LANES, tokens)).T
    earlier = jnp.zeros((1, tokens), jnp.int32)
    for start in range(0, tokens, LANES):
        rows = min(LANES, tokens - start)
        shape = (rows, tokens)
        same = tiled_lanes(ids_column[start : start + rows], tokens) == ids
        before = lax.broadcasted_iota(jnp.int32, shape, 0) + start < lax.broadcasted_iota(
            jnp.int32, shape, 1
        )
        earlier = earlier + jnp.sum(
            jnp.where(same & before, 1, 0), axis=0, keepdims=True
        )
    slots = ids * capacity + earlier
    slot_row[...] = slots
    slot_column[...] = jnp.broadcast_to(slots, (LANES, tokens)).T
    load_grad.wait()

    def rows_of(pair):
        return pl.ds(pl.multiple_of(pair * both, 16), both)

    def pack(pair, target):
        far, near = steps_of(pair, groups)
        chosen = []
        for step, size in ((far, far_rows), (near, capacity)):
            row = lax.broadcasted_iota(jnp.int32, (size, tokens), 0)
            wanted = row + across(me, step, groups) * capacity
            chosen.append(jnp.where(slot_row[...] == wanted, 1.0, 0.0))
        pick = jnp.concatenate(chosen, axis=0).astype(jnp.bfloat16)
        rows = jnp.dot(pick, grad[...], preferred_element_type=jnp.float32)
        target[rows_of(pair), :] = rows.astype(jnp.bfloat16)

    def sent_rows(slot, kind):
        pair = lax.div(slot, 2)
        if kind is FAR:
            return pl.ds(pl.multiple_of(pair * both, 16), far_rows)
        return pl.ds(pl.multiple_of(pair * both + far_rows, 16), capacity)

    def outward(slot, step, kind=None):
        return pltpu.make_async_remote_copy(
            src_ref=outgoing.at[sent_rows(slot, kind)],
            dst_ref=arrived.at[part, sent_rows(slot, kind)],
            send_sem=send_sem.at[slot],
            recv_sem=recv_sem.at[slot],
            device_id=(across(me, step, groups), part),
            device_id_type=MESH,
        )

    def sideways(pair, hop, rows=None):
        rows = rows_of(pair) if rows is None else rows
        return pltpu.make_async_remote_copy(
            src_ref=arrived.at[part, rows],
            dst_ref=arrived.at[part, rows],
            send_sem=peer_send_sem.at[hop - 1, pair],
            recv_sem=peer_recv_sem.at[hop - 1, pair],
            device_id=(me, lax.rem(part + hop, parts)),
            device_id_type=MESH,
        )

    def sideways_in(pair, hop, rows=None):
        rows = rows_of(pair) if rows is None else rows
        sender = lax.rem(part + parts - hop, parts)
        return pltpu.make_async_remote_copy(
            src_ref=arrived.at[sender, rows],
            dst_ref=arrived.at[sender, rows],
            send_sem=peer_send_sem.at[hop - 1, pair],
            recv_sem=peer_recv_sem.at[hop - 1, pair],
            device_id=(me, lax.rem(part + hop, parts)),
            device_id_type=MESH,
        )

    def homeward(slot, step, kind=None):
        return pltpu.make_async_remote_copy(
            src_ref=product.at[sent_rows(slot, kind)],
            dst_ref=returned.at[sent_rows(slot, kind)],
            send_sem=back_send_sem.at[slot],
            recv_sem=back_recv_sem.at[slot],
            device_id=(across(me, step, groups), part),
            device_id_type=MESH,
        )

    own = pairs - 1
    own_rows = pl.ds(own * both + far_rows, capacity)

    def send_pair(pair):
        far, near = steps_of(pair, groups)
        outward(2 * pair, far, FAR).start()

        @pl.when(pair < own)
        def _():
            outward(2 * pair + 1, near).start()

    if spill:
        mirror = (across(me, middle, groups), part)

        def to_mirror(source, target, sems):
            return pltpu.make_async_remote_copy(
                src_ref=source,
                dst_ref=target,
                send_sem=sems.at[0],
                recv_sem=sems.at[1],
                device_id=mirror,
                device_id_type=MESH,
            )

        def send_count(step):
            return pltpu.make_async_remote_copy(
                src_ref=counts.at[0],
                dst_ref=counts.at[step],
                send_sem=count_send_sem.at[step],
                recv_sem=count_recv_sem.at[step],
                device_id=(across(me, step, groups), part),
                device_id_type=MESH,
            )

        def half_rows(index):
            return pl.ds(pl.multiple_of(index * half, half), half)

        relay_rows = pl.ds(pairs * both, relayed)
        own_relay = pl.ds(pairs * both, half)

        def relay_at(step):
            return pl.ds(pl.multiple_of(pairs * both + step * half, 16), half)

        def relay(step):
            target = across(me, step, groups)
            return pltpu.make_async_remote_copy(
                src_ref=relay_out.at[half_rows(target - side * middle)],
                dst_ref=arrived.at[part, relay_at(step)],
                send_sem=relay_send_sem.at[step],
                recv_sem=relay_recv_sem.at[step],
                device_id=(target, part),
                device_id_type=MESH,
            )

        def relay_home(step):
            return pltpu.make_async_remote_copy(
                src_ref=product.at[relay_at(step)],
                dst_ref=relay_back.at[half_rows(local)],
                send_sem=relay_back_send_sem.at[step],
                recv_sem=relay_back_recv_sem.at[step],
                device_id=(across(me, step, groups), part),
                device_id_type=MESH,
            )

        def relay_home_in(step):
            sender = across(me, step, groups) - side * middle
            return pltpu.make_async_remote_copy(
                src_ref=product.at[relay_at(step)],
                dst_ref=relay_back.at[half_rows(sender)],
                send_sem=relay_back_send_sem.at[step],
                recv_sem=relay_back_recv_sem.at[step],
                device_id=(across(me, step, groups), part),
                device_id_type=MESH,
            )

        place_copy = to_mirror(place_out, place_in, place_sem)
        spill_copy = to_mirror(spill_out, spill_in.at[pl.ds(0, spill)], spill_sem)
        spill_back_copy = to_mirror(
            spill_back, spill_home.at[pl.ds(0, spill)], spill_back_sem
        )
        early = 3 * pairs // 8
        pack(0, outgoing)
        pl.semaphore_wait(barrier, groups - 1 + parts - 1)
        send_pair(0)
        expert_side = jnp.where(ids >= middle, 1, 0)
        over = jnp.where((expert_side != side) & (earlier >= half), 1, 0)
        over_column = jnp.broadcast_to(over, (LANES, tokens)).T
        order = jnp.zeros((1, tokens), jnp.int32)
        for start in range(0, tokens, LANES):
            rows = min(LANES, tokens - start)
            shape = (rows, tokens)
            before = lax.broadcasted_iota(jnp.int32, shape, 0) + start < lax.broadcasted_iota(
                jnp.int32, shape, 1
            )
            ahead = tiled_lanes(over_column[start : start + rows], tokens)
            order = order + jnp.sum(jnp.where(before, ahead, 0), axis=0, keepdims=True)
        order = jnp.where(over > 0, order, -1)
        spill_column[...] = jnp.broadcast_to(order, (LANES, tokens)).T
        spot = (ids - expert_side * middle) * half + earlier - half + 1
        spot_column = jnp.broadcast_to(spot, (LANES, tokens)).T
        match = tiled_lanes(spill_column[...], lanes) == lax.broadcasted_iota(
            jnp.int32, (tokens, lanes), 1
        )
        place_out[...] = (
            jnp.sum(
                jnp.where(match, tiled_lanes(spot_column, lanes), 0), axis=0, keepdims=True
            )
            - 1
        )
        counts[0] = jnp.broadcast_to(jnp.sum(over, axis=1, keepdims=True), (1, LANES))
        spill_in[spill:, :] = jnp.zeros((lanes - spill, width), jnp.bfloat16)
        spill_home[spill:, :] = jnp.zeros((lanes - spill, units), jnp.bfloat16)
        index = lax.broadcasted_iota(jnp.int32, (spill, tokens), 0)
        pick = jnp.where(order == index, 1.0, 0.0).astype(jnp.bfloat16)
        spill_out[...] = jnp.dot(
            pick, grad[...], preferred_element_type=jnp.float32
        ).astype(jnp.bfloat16)
        place_copy.start()
        spill_copy.start()

        @pl.loop(1, max(early, 1))
        def _(pair):
            pack(pair, outgoing)
            send_pair(pair)

        place_copy.wait_recv()
        spill_copy.wait_recv()
        index = lax.broadcasted_iota(jnp.int32, (relayed, lanes), 0)
        pick = jnp.where(place_in[...] == index, 1.0, 0.0).astype(jnp.bfloat16)
        relay_out[...] = jnp.dot(
            pick, spill_in[...], preferred_element_type=jnp.float32
        ).astype(jnp.bfloat16)

        @pl.loop(1, middle)
        def _(step):
            relay(step).start()

        arrived[part, own_relay, :] = relay_out[half_rows(local), :]

        @pl.loop(max(early, 1), pairs)
        def _(pair):
            pack(pair, outgoing)
            send_pair(pair)

        @pl.loop(1, groups)
        def _(step):
            send_count(step).start()

    else:
        pack(0, outgoing)
        pl.semaphore_wait(barrier, groups - 1 + parts - 1)
        send_pair(0)

        @pl.loop(1, pairs)
        def _(pair):
            pack(pair, outgoing)
            send_pair(pair)

    arrived[part, own_rows, :] = outgoing[own_rows, :]

    def multiply(rows):
        @pl.loop(0, units // tile)
        def _(block):
            columns = pl.ds(pl.multiple_of(block * tile, tile), tile)
            value = jnp.zeros((rows.size, tile), jnp.float32)
            for piece in range(parts):
                value = value + lax.dot_general(
                    arrived[piece, rows, :],
                    weight[columns, piece * width : (piece + 1) * width],
                    (((1,), (1,)), ((), ())),
                    preferred_element_type=jnp.float32,
                )
            product[rows, columns] = value.astype(jnp.bfloat16)

    if spill:

        def multiply_relayed():
            @pl.loop(1, middle)
            def _(step):
                relay(step).wait_recv()

            for hop in range(1, parts):
                sideways(pairs, hop, relay_rows).start()
            for hop in range(1, parts):
                sideways_in(pairs, hop, relay_rows).wait_recv()
            multiply(relay_rows)

            @pl.loop(1, middle)
            def _(step):
                relay_home(step).start()

        def pack_home():
            relay_back[half_rows(local), :] = product[own_relay, :]

            @pl.loop(1, middle)
            def _(step):
                relay_home_in(step).wait_recv()

            column = jnp.broadcast_to(place_in[...], (LANES, lanes)).T[:spill]
            index = lax.broadcasted_iota(jnp.int32, (spill, relayed), 1)
            wide = jnp.concatenate([column] * -(-relayed // LANES), axis=1)
            pick = jnp.where(wide[:, : relayed] == index, 1.0, 0.0).astype(jnp.bfloat16)

            @pl.loop(0, units // tile)
            def _(block):
                columns = pl.ds(pl.multiple_of(block * tile, tile), tile)
                spill_back[:, columns] = jnp.dot(
                    pick, relay_back[:, columns], preferred_element_type=jnp.float32
                ).astype(jnp.bfloat16)

            spill_back_copy.start()

    @pl.loop(0, pairs + 1)
    def _(turn):
        @pl.when(turn < pairs)
        def _():
            far, near = steps_of(turn, groups)
            outward(2 * turn, far, FAR).wait_recv()

            @pl.when(turn < own)
            def _():
                outward(2 * turn + 1, near).wait_recv()

            for hop in range(1, parts):
                sideways(turn, hop).start()

        @pl.when(turn == 0)
        def _():
            load_weight.wait()

        @pl.when(turn > 0)
        def _():
            pair = turn - 1
            for hop in range(1, parts):
                sideways_in(pair, hop).wait_recv()
            multiply(rows_of(pair))
            far, near = steps_of(pair, groups)
            homeward(2 * pair, far, FAR).start()

            @pl.when(pair < own)
            def _():
                homeward(2 * pair + 1, near).start()

        if spill:

            @pl.when(turn == max(early, 1))
            def _():
                multiply_relayed()

            @pl.when(turn == own)
            def _():
                pack_home()

    returned[own_rows, :] = product[own_rows, :]
    load_hidden.wait()
    total[...] = jnp.zeros_like(total)
    sums[...] = jnp.zeros_like(sums)

    def placement(pair, rows):
        far, near = steps_of(pair, groups)
        lane = lax.broadcasted_iota(jnp.int32, (1, both), 1)
        wanted = jnp.where(
            lane < far_rows,
            lane + across(me, far, groups) * capacity,
            lane + across(me, near, groups) * capacity - far_rows,
        )
        hit = slot_column[rows, :both] == wanted
        return jnp.where(hit, 1.0, 0.0).astype(jnp.bfloat16)

    def wait_home(pair):
        far, near = steps_of(pair, groups)
        homeward(2 * pair, far, FAR).wait_recv()

        @pl.when(pair < own)
        def _():
            homeward(2 * pair + 1, near).wait_recv()

    everything = pl.ds(0, tokens)

    def gather(place, source, rows):
        @pl.loop(0, units // tile)
        def _(block):
            columns = pl.ds(pl.multiple_of(block * tile, tile), tile)
            total[:, columns] += jnp.dot(
                place, source[rows, columns], preferred_element_type=jnp.float32
            )

    @pl.loop(0, own)
    def _(pair):
        wait_home(pair)
        gather(placement(pair, everything), returned, rows_of(pair))

    if spill:
        spill_back_copy.wait_recv()
        lane = lax.broadcasted_iota(jnp.int32, (tokens, lanes), 1)
        hit = tiled_lanes(spill_column[...], lanes) == lane
        gather(jnp.where(hit, 1.0, 0.0).astype(jnp.bfloat16), spill_home, pl.ds(0, lanes))
    wait_home(own)
    chunk = min(LANES, tokens)

    @pl.loop(0, tokens // chunk)
    def _(part_of):
        rows = pl.ds(pl.multiple_of(part_of * chunk, chunk), chunk)
        place = placement(own, rows)

        @pl.loop(0, units // tile)
        def _(block):
            columns = pl.ds(pl.multiple_of(block * tile, tile), tile)
            back = total[rows, columns] + jnp.dot(
                place, returned[rows_of(own), columns], preferred_element_type=jnp.float32
            )
            out_ref[rows, columns] = back.astype(jnp.bfloat16)
            terms = hidden[rows, columns].astype(jnp.float32) * back
            sums[rows, :] += sum(
                terms[:, at : at + LANES] for at in range(0, tile, LANES)
            )

    row = jnp.sum(sums[...].T, axis=0, keepdims=True)
    gate_sums[part] = jnp.broadcast_to(row, (8, tokens))

    def gate_copy(hop, sender):
        return pltpu.make_async_remote_copy(
            src_ref=gate_sums.at[sender],
            dst_ref=gate_sums.at[sender],
            send_sem=gate_send_sem.at[hop - 1],
            recv_sem=gate_recv_sem.at[hop - 1],
            device_id=(me, lax.rem(part + hop, parts)),
            device_id_type=MESH,
        )

    for hop in range(1, parts):
        gate_copy(hop, part).start()

    @pl.loop(0, pairs)
    def _(pair):
        far, near = steps_of(pair, groups)
        outward(2 * pair, far, FAR).wait_send()
        homeward(2 * pair, far, FAR).wait_send()
        for hop in range(1, parts):
            sideways(pair, hop).wait_send()

        @pl.when(pair < own)
        def _():
            outward(2 * pair + 1, near).wait_send()
            homeward(2 * pair + 1, near).wait_send()

    if spill:
        for hop in range(1, parts):
            sideways(pairs, hop, relay_rows).wait_send()
        place_copy.wait_send()
        spill_copy.wait_send()
        spill_back_copy.wait_send()

        @pl.loop(1, middle)
        def _(step):
            relay(step).wait_send()
            relay_home(step).wait_send()

        @pl.loop(1, groups)
        def _(step):
            send_count(step).wait()

        most_ref[...] = jnp.max(counts[...], axis=0)
    else:
        most_ref[...] = jnp.zeros_like(most_ref)
    for hop in range(1, parts):
        gate_copy(hop, part).wait_send()
        gate_copy(hop, lax.rem(part + parts - hop, parts)).wait_recv()
    result = gate_sums[0]
    for piece in range(1, parts):
        result = result + gate_sums[piece]
    gate_out_ref[...] = result[:1]


def call(groups, parts, capacity, spill, grad_out, hidden_in, ids, w_down):
    tokens, width = grad_out.shape
    units, features = w_down.shape
    tile = min(512, units)
    rows = groups * capacity * 3 // 4 if spill else groups * capacity
    dma = pltpu.SemaphoreType.DMA
    hops = max(parts - 1, 1)
    middle = groups // 2
    lanes = -(-spill // LANES) * LANES
    relayed = middle * capacity // 2
    extra = relayed if spill else 0
    spill_scratch = [
        pltpu.VMEM((tokens, LANES), jnp.int32),
        pltpu.VMEM((1, lanes), jnp.int32),
        pltpu.VMEM((1, lanes), jnp.int32),
        pltpu.VMEM((groups, 1, LANES), jnp.int32),
        pltpu.VMEM((spill, width), jnp.bfloat16),
        pltpu.VMEM((lanes, width), jnp.bfloat16),
        pltpu.VMEM((relayed, width), jnp.bfloat16),
        pltpu.VMEM((relayed, units), jnp.bfloat16),
        pltpu.VMEM((spill, units), jnp.bfloat16),
        pltpu.VMEM((lanes, units), jnp.bfloat16),
        dma((2,)),
        dma((groups,)),
        dma((groups,)),
        dma((2,)),
        dma((middle,)),
        dma((middle,)),
        dma((middle,)),
        dma((middle,)),
        dma((2,)),
    ]
    return pl.pallas_call(
        functools.partial(kernel, groups, parts, capacity, tile, spill),
        out_shape=(
            jax.ShapeDtypeStruct((tokens, units), jnp.bfloat16),
            jax.ShapeDtypeStruct((1, tokens), jnp.float32),
            jax.ShapeDtypeStruct((1, LANES), jnp.int32),
        ),
        in_specs=[
            pl.BlockSpec(memory_space=pl.ANY),
            pl.BlockSpec(memory_space=pl.ANY),
            pl.BlockSpec(memory_space=pltpu.VMEM),
            pl.BlockSpec(memory_space=pl.ANY),
        ],
        out_specs=(pl.BlockSpec(memory_space=pltpu.VMEM),) * 3,
        scratch_shapes=[
            pltpu.VMEM((tokens, width), jnp.bfloat16),
            pltpu.VMEM((tokens, units), jnp.bfloat16),
            pltpu.VMEM((units, features), jnp.bfloat16),
            pltpu.VMEM((rows, width), jnp.bfloat16),
            pltpu.VMEM((parts, rows + extra, width), jnp.bfloat16),
            pltpu.VMEM((rows + extra, units), jnp.bfloat16),
            pltpu.VMEM((rows, units), jnp.bfloat16),
            pltpu.VMEM((tokens, units), jnp.float32),
            pltpu.VMEM((1, tokens), jnp.int32),
            pltpu.VMEM((tokens, LANES), jnp.int32),
            pltpu.VMEM((tokens, LANES), jnp.float32),
            pltpu.VMEM((parts, 8, tokens), jnp.float32),
            dma((3,)),
            dma((groups,)),
            dma((groups,)),
            dma((hops, groups // 2 + 1)),
            dma((hops, groups // 2 + 1)),
            dma((groups,)),
            dma((groups,)),
            dma((hops,)),
            dma((hops,)),
        ]
        + (spill_scratch if spill else []),
        compiler_params=pltpu.CompilerParams(
            collective_id=1 if spill else 0,
            has_side_effects=True,
            vmem_limit_bytes=56 * 1024 * 1024,
        ),
    )(grad_out, hidden_in, ids, w_down)


def body(groups, parts, grad_out, hidden_in, gate_prob, expert_ids, w_down):
    tokens = grad_out.shape[0]
    experts, units, features = w_down.shape
    capacity = 2 * tokens // (groups * experts)
    args = (grad_out, hidden_in, expert_ids.reshape(1, tokens), w_down.reshape(units, features))
    whole = functools.partial(call, groups, parts, capacity, 0)
    spill = 9 * groups * capacity // 64 // 16 * 16
    if capacity % 32 == 0:
        back, gate_sum, most = call(groups, parts, capacity, spill, *args)
        back, gate_sum = lax.cond(
            most[0, 0] > spill,
            lambda back, gate_sum: whole(*args)[:2],
            lambda back, gate_sum: (back, gate_sum),
            back,
            gate_sum,
        )
    else:
        back, gate_sum, _ = whole(*args)
    grad_hidden = (gate_prob[:, None] * back.astype(jnp.float32)).astype(jnp.bfloat16)
    return grad_hidden, gate_sum.reshape(tokens)


def solution(mesh):
    return jax.shard_map(
        functools.partial(body, mesh.shape["expert"], mesh.shape["tensor"]),
        mesh=mesh,
        in_specs=(
            P("expert", "tensor"),
            P("expert", "tensor"),
            P("expert"),
            P("expert", None),
            P("expert", "tensor", None),
        ),
        out_specs=(P("expert", "tensor"), P("expert")),
        check_vma=False,
    )
```

```python
import functools

import jax
import jax.numpy as jnp
from jax import lax
from jax.experimental import pallas as pl
from jax.experimental.pallas import tpu as pltpu
from jax.sharding import PartitionSpec as P

MESH = pl.DeviceIdType.MESH
LANES = 128
FAR = "far"


def across(index, step, count):
    total, bit = 0, 1
    while bit < count:
        total = total + lax.rem(lax.div(index, bit) + lax.div(step, bit), 2) * bit
        bit *= 2
    return total


def steps_of(pair, groups):
    quarter = groups // 4
    near = jnp.where(pair < quarter, quarter + pair, lax.rem(pair + 1, quarter))
    return groups // 2 + pair, near


def tiled_lanes(column, width):
    return jnp.concatenate([column] * (width // LANES), axis=1)


def kernel(
    groups,
    parts,
    capacity,
    tile,
    spill,
    grad_ref,
    hidden_ref,
    ids_ref,
    w_ref,
    out_ref,
    gate_out_ref,
    most_ref,
    grad,
    hidden,
    weight,
    outgoing,
    arrived,
    product,
    returned,
    total,
    slot_row,
    slot_column,
    sums,
    gate_sums,
    local_sem,
    send_sem,
    recv_sem,
    peer_send_sem,
    peer_recv_sem,
    back_send_sem,
    back_recv_sem,
    gate_send_sem,
    gate_recv_sem,
    *spill_refs,
):
    me = lax.axis_index("expert")
    part = lax.axis_index("tensor")
    pairs = groups // 2
    tokens, width = grad.shape
    units = weight.shape[0]
    middle = groups // 2
    half = capacity // 2
    side = lax.div(me, middle)
    local = me - side * middle
    if spill:
        (
            spill_column,
            place_out,
            place_in,
            counts,
            spill_out,
            spill_in,
            relay_out,
            relay_back,
            spill_back,
            spill_home,
            place_sem,
            count_send_sem,
            count_recv_sem,
            spill_sem,
            relay_send_sem,
            relay_recv_sem,
            relay_back_send_sem,
            relay_back_recv_sem,
            spill_back_sem,
        ) = spill_refs
        lanes = place_in.shape[1]
    far_rows = half if spill else capacity
    both = far_rows + capacity
    span = 2 if pairs % 2 == 0 else 1
    blocks = pairs // span
    last = blocks - 1
    relayed = middle * half

    load_grad = pltpu.make_async_copy(grad_ref, grad, local_sem.at[0])
    load_weight = pltpu.make_async_copy(w_ref, weight, local_sem.at[1])
    load_hidden = pltpu.make_async_copy(hidden_ref, hidden, local_sem.at[2])
    load_grad.start()
    load_weight.start()
    load_hidden.start()

    barrier = pltpu.get_barrier_semaphore()

    @pl.loop(1, groups)
    def _(step):
        pl.semaphore_signal(
            barrier, inc=1, device_id=(across(me, step, groups), part), device_id_type=MESH
        )

    for hop in range(1, parts):
        pl.semaphore_signal(
            barrier, inc=1, device_id=(me, lax.rem(part + hop, parts)), device_id_type=MESH
        )

    ids = ids_ref[...]
    ids_column = jnp.broadcast_to(ids, (LANES, tokens)).T
    earlier = jnp.zeros((1, tokens), jnp.int32)
    for start in range(0, tokens, LANES):
        rows = min(LANES, tokens - start)
        shape = (rows, tokens)
        same = tiled_lanes(ids_column[start : start + rows], tokens) == ids
        before = lax.broadcasted_iota(jnp.int32, shape, 0) + start < lax.broadcasted_iota(
            jnp.int32, shape, 1
        )
        earlier = earlier + jnp.sum(
            jnp.where(same & before, 1, 0), axis=0, keepdims=True
        )
    slots = ids * capacity + earlier
    slot_row[...] = slots
    slot_column[...] = jnp.broadcast_to(slots, (LANES, tokens)).T
    load_grad.wait()

    def rows_of(block):
        return pl.ds(pl.multiple_of(block * span * both, 16), span * both)

    def segments(block):
        found = []
        for inner in range(span):
            far, near = steps_of(block * span + inner, groups)
            found.append((far, inner * both, far_rows))
            found.append((near, inner * both + far_rows, capacity))
        return found

    def pack(block, target):
        chosen = []
        for step, _, size in segments(block):
            row = lax.broadcasted_iota(jnp.int32, (size, tokens), 0)
            wanted = row + across(me, step, groups) * capacity
            chosen.append(jnp.where(slot_row[...] == wanted, 1.0, 0.0))
        pick = jnp.concatenate(chosen, axis=0).astype(jnp.bfloat16)
        rows = jnp.dot(pick, grad[...], preferred_element_type=jnp.float32)
        target[rows_of(block), :] = rows.astype(jnp.bfloat16)

    def sent_rows(slot, kind):
        pair = lax.div(slot, 2)
        if kind is FAR:
            return pl.ds(pl.multiple_of(pair * both, 16), far_rows)
        return pl.ds(pl.multiple_of(pair * both + far_rows, 16), capacity)

    def outward(slot, step, kind=None):
        return pltpu.make_async_remote_copy(
            src_ref=outgoing.at[sent_rows(slot, kind)],
            dst_ref=arrived.at[part, sent_rows(slot, kind)],
            send_sem=send_sem.at[slot],
            recv_sem=recv_sem.at[slot],
            device_id=(across(me, step, groups), part),
            device_id_type=MESH,
        )

    def sideways(block, hop, rows=None):
        rows = rows_of(block) if rows is None else rows
        return pltpu.make_async_remote_copy(
            src_ref=arrived.at[part, rows],
            dst_ref=arrived.at[part, rows],
            send_sem=peer_send_sem.at[hop - 1, block],
            recv_sem=peer_recv_sem.at[hop - 1, block],
            device_id=(me, lax.rem(part + hop, parts)),
            device_id_type=MESH,
        )

    def sideways_in(block, hop, rows=None):
        rows = rows_of(block) if rows is None else rows
        sender = lax.rem(part + parts - hop, parts)
        return pltpu.make_async_remote_copy(
            src_ref=arrived.at[sender, rows],
            dst_ref=arrived.at[sender, rows],
            send_sem=peer_send_sem.at[hop - 1, block],
            recv_sem=peer_recv_sem.at[hop - 1, block],
            device_id=(me, lax.rem(part + hop, parts)),
            device_id_type=MESH,
        )

    def homeward(slot, step, kind=None):
        return pltpu.make_async_remote_copy(
            src_ref=product.at[sent_rows(slot, kind)],
            dst_ref=returned.at[sent_rows(slot, kind)],
            send_sem=back_send_sem.at[slot],
            recv_sem=back_recv_sem.at[slot],
            device_id=(across(me, step, groups), part),
            device_id_type=MESH,
        )

    own = pairs - 1
    own_rows = pl.ds(own * both + far_rows, capacity)

    def each_pair(block, copy, act):
        for inner in range(span):
            pair = block * span + inner
            far, near = steps_of(pair, groups)
            act(copy(2 * pair, far, FAR))

            @pl.when(pair < own)
            def _():
                act(copy(2 * pair + 1, near))

    def send_block(block):
        each_pair(block, outward, lambda copy: copy.start())

    if spill:
        mirror = (across(me, middle, groups), part)

        def to_mirror(source, target, sems):
            return pltpu.make_async_remote_copy(
                src_ref=source,
                dst_ref=target,
                send_sem=sems.at[0],
                recv_sem=sems.at[1],
                device_id=mirror,
                device_id_type=MESH,
            )

        def send_count(step):
            return pltpu.make_async_remote_copy(
                src_ref=counts.at[0],
                dst_ref=counts.at[step],
                send_sem=count_send_sem.at[step],
                recv_sem=count_recv_sem.at[step],
                device_id=(across(me, step, groups), part),
                device_id_type=MESH,
            )

        def half_rows(index):
            return pl.ds(pl.multiple_of(index * half, half), half)

        relay_rows = pl.ds(pairs * both, relayed)
        own_relay = pl.ds(pairs * both, half)

        def relay_at(step):
            return pl.ds(pl.multiple_of(pairs * both + step * half, 16), half)

        def relay(step):
            target = across(me, step, groups)
            return pltpu.make_async_remote_copy(
                src_ref=relay_out.at[half_rows(target - side * middle)],
                dst_ref=arrived.at[part, relay_at(step)],
                send_sem=relay_send_sem.at[step],
                recv_sem=relay_recv_sem.at[step],
                device_id=(target, part),
                device_id_type=MESH,
            )

        def relay_home(step):
            return pltpu.make_async_remote_copy(
                src_ref=product.at[relay_at(step)],
                dst_ref=relay_back.at[half_rows(local)],
                send_sem=relay_back_send_sem.at[step],
                recv_sem=relay_back_recv_sem.at[step],
                device_id=(across(me, step, groups), part),
                device_id_type=MESH,
            )

        def relay_home_in(step):
            sender = across(me, step, groups) - side * middle
            return pltpu.make_async_remote_copy(
                src_ref=product.at[relay_at(step)],
                dst_ref=relay_back.at[half_rows(sender)],
                send_sem=relay_back_send_sem.at[step],
                recv_sem=relay_back_recv_sem.at[step],
                device_id=(across(me, step, groups), part),
                device_id_type=MESH,
            )

        place_copy = to_mirror(place_out, place_in, place_sem)
        spill_copy = to_mirror(spill_out, spill_in.at[pl.ds(0, spill)], spill_sem)
        spill_back_copy = to_mirror(
            spill_back, spill_home.at[pl.ds(0, spill)], spill_back_sem
        )
        early = (blocks + 1) // 2
        pack(0, outgoing)
        pl.semaphore_wait(barrier, groups - 1 + parts - 1)
        send_block(0)
        expert_side = jnp.where(ids >= middle, 1, 0)
        over = jnp.where((expert_side != side) & (earlier >= half), 1, 0)
        over_column = jnp.broadcast_to(over, (LANES, tokens)).T
        order = jnp.zeros((1, tokens), jnp.int32)
        for start in range(0, tokens, LANES):
            rows = min(LANES, tokens - start)
            shape = (rows, tokens)
            before = lax.broadcasted_iota(jnp.int32, shape, 0) + start < lax.broadcasted_iota(
                jnp.int32, shape, 1
            )
            ahead = tiled_lanes(over_column[start : start + rows], tokens)
            order = order + jnp.sum(jnp.where(before, ahead, 0), axis=0, keepdims=True)
        order = jnp.where(over > 0, order, -1)
        spill_column[...] = jnp.broadcast_to(order, (LANES, tokens)).T
        spot = (ids - expert_side * middle) * half + earlier - half + 1
        spot_column = jnp.broadcast_to(spot, (LANES, tokens)).T
        match = tiled_lanes(spill_column[...], lanes) == lax.broadcasted_iota(
            jnp.int32, (tokens, lanes), 1
        )
        place_out[...] = (
            jnp.sum(
                jnp.where(match, tiled_lanes(spot_column, lanes), 0), axis=0, keepdims=True
            )
            - 1
        )
        counts[0] = jnp.broadcast_to(jnp.sum(over, axis=1, keepdims=True), (1, LANES))
        spill_in[spill:, :] = jnp.zeros((lanes - spill, width), jnp.bfloat16)
        spill_home[spill:, :] = jnp.zeros((lanes - spill, units), jnp.bfloat16)
        index = lax.broadcasted_iota(jnp.int32, (spill, tokens), 0)
        pick = jnp.where(order == index, 1.0, 0.0).astype(jnp.bfloat16)
        spill_out[...] = jnp.dot(
            pick, grad[...], preferred_element_type=jnp.float32
        ).astype(jnp.bfloat16)
        place_copy.start()
        spill_copy.start()

        @pl.loop(1, early)
        def _(block):
            pack(block, outgoing)
            send_block(block)

        place_copy.wait_recv()
        spill_copy.wait_recv()
        index = lax.broadcasted_iota(jnp.int32, (relayed, lanes), 0)
        pick = jnp.where(place_in[...] == index, 1.0, 0.0).astype(jnp.bfloat16)
        relay_out[...] = jnp.dot(
            pick, spill_in[...], preferred_element_type=jnp.float32
        ).astype(jnp.bfloat16)

        @pl.loop(1, middle)
        def _(step):
            relay(step).start()

        arrived[part, own_relay, :] = relay_out[half_rows(local), :]

        @pl.loop(early, blocks)
        def _(block):
            pack(block, outgoing)
            send_block(block)

        @pl.loop(1, groups)
        def _(step):
            send_count(step).start()

    else:
        pack(0, outgoing)
        pl.semaphore_wait(barrier, groups - 1 + parts - 1)
        send_block(0)

        @pl.loop(1, blocks)
        def _(block):
            pack(block, outgoing)
            send_block(block)

    arrived[part, own_rows, :] = outgoing[own_rows, :]

    def multiply(rows):
        @pl.loop(0, units // tile)
        def _(block):
            columns = pl.ds(pl.multiple_of(block * tile, tile), tile)
            value = jnp.zeros((rows.size, tile), jnp.float32)
            for piece in range(parts):
                value = value + lax.dot_general(
                    arrived[piece, rows, :],
                    weight[columns, piece * width : (piece + 1) * width],
                    (((1,), (1,)), ((), ())),
                    preferred_element_type=jnp.float32,
                )
            product[rows, columns] = value.astype(jnp.bfloat16)

    if spill:

        def multiply_relayed():
            @pl.loop(1, middle)
            def _(step):
                relay(step).wait_recv()

            for hop in range(1, parts):
                sideways(blocks, hop, relay_rows).start()
            for hop in range(1, parts):
                sideways_in(blocks, hop, relay_rows).wait_recv()
            multiply(relay_rows)

            @pl.loop(1, middle)
            def _(step):
                relay_home(step).start()

        def pack_home():
            relay_back[half_rows(local), :] = product[own_relay, :]

            @pl.loop(1, middle)
            def _(step):
                relay_home_in(step).wait_recv()

            column = jnp.broadcast_to(place_in[...], (LANES, lanes)).T[:spill]
            index = lax.broadcasted_iota(jnp.int32, (spill, relayed), 1)
            wide = jnp.concatenate([column] * -(-relayed // LANES), axis=1)
            pick = jnp.where(wide[:, : relayed] == index, 1.0, 0.0).astype(jnp.bfloat16)

            @pl.loop(0, units // tile)
            def _(block):
                columns = pl.ds(pl.multiple_of(block * tile, tile), tile)
                spill_back[:, columns] = jnp.dot(
                    pick, relay_back[:, columns], preferred_element_type=jnp.float32
                ).astype(jnp.bfloat16)

            spill_back_copy.start()

    @pl.loop(0, blocks + 1)
    def _(turn):
        @pl.when(turn < blocks)
        def _():
            each_pair(turn, outward, lambda copy: copy.wait_recv())
            for hop in range(1, parts):
                sideways(turn, hop).start()

        @pl.when(turn == 0)
        def _():
            load_weight.wait()

        @pl.when(turn > 0)
        def _():
            for hop in range(1, parts):
                sideways_in(turn - 1, hop).wait_recv()
            multiply(rows_of(turn - 1))
            each_pair(turn - 1, homeward, lambda copy: copy.start())

        if spill:

            @pl.when(turn == early)
            def _():
                multiply_relayed()

            @pl.when(turn == max(last, early))
            def _():
                pack_home()

    returned[own_rows, :] = product[own_rows, :]
    load_hidden.wait()
    total[...] = jnp.zeros_like(total)
    sums[...] = jnp.zeros_like(sums)

    def placement(block, rows):
        lane = lax.broadcasted_iota(jnp.int32, (1, span * both), 1)
        wanted = lane
        for step, first, _ in segments(block):
            base = across(me, step, groups) * capacity - first
            wanted = jnp.where(lane >= first, lane + base, wanted)
        column = jnp.concatenate([slot_column[rows, :]] * -(-span * both // LANES), axis=1)
        hit = column[:, : span * both] == wanted
        return jnp.where(hit, 1.0, 0.0).astype(jnp.bfloat16)

    def wait_home(block):
        each_pair(block, homeward, lambda copy: copy.wait_recv())

    everything = pl.ds(0, tokens)

    def gather(place, source, rows):
        @pl.loop(0, units // tile)
        def _(block):
            columns = pl.ds(pl.multiple_of(block * tile, tile), tile)
            total[:, columns] += jnp.dot(
                place, source[rows, columns], preferred_element_type=jnp.float32
            )

    @pl.loop(0, last)
    def _(block):
        wait_home(block)
        gather(placement(block, everything), returned, rows_of(block))

    if spill:
        spill_back_copy.wait_recv()
        lane = lax.broadcasted_iota(jnp.int32, (tokens, lanes), 1)
        hit = tiled_lanes(spill_column[...], lanes) == lane
        gather(jnp.where(hit, 1.0, 0.0).astype(jnp.bfloat16), spill_home, pl.ds(0, lanes))
    wait_home(last)
    chunk = min(LANES, tokens)

    @pl.loop(0, tokens // chunk)
    def _(part_of):
        rows = pl.ds(pl.multiple_of(part_of * chunk, chunk), chunk)
        place = placement(last, rows)

        @pl.loop(0, units // tile)
        def _(block):
            columns = pl.ds(pl.multiple_of(block * tile, tile), tile)
            back = total[rows, columns] + jnp.dot(
                place, returned[rows_of(last), columns], preferred_element_type=jnp.float32
            )
            out_ref[rows, columns] = back.astype(jnp.bfloat16)
            terms = hidden[rows, columns].astype(jnp.float32) * back
            sums[rows, :] += sum(
                terms[:, at : at + LANES] for at in range(0, tile, LANES)
            )

    row = jnp.sum(sums[...].T, axis=0, keepdims=True)
    gate_sums[part] = jnp.broadcast_to(row, (8, tokens))

    def gate_copy(hop, sender):
        return pltpu.make_async_remote_copy(
            src_ref=gate_sums.at[sender],
            dst_ref=gate_sums.at[sender],
            send_sem=gate_send_sem.at[hop - 1],
            recv_sem=gate_recv_sem.at[hop - 1],
            device_id=(me, lax.rem(part + hop, parts)),
            device_id_type=MESH,
        )

    for hop in range(1, parts):
        gate_copy(hop, part).start()

    @pl.loop(0, blocks)
    def _(block):
        each_pair(block, outward, lambda copy: copy.wait_send())
        each_pair(block, homeward, lambda copy: copy.wait_send())
        for hop in range(1, parts):
            sideways(block, hop).wait_send()

    if spill:
        for hop in range(1, parts):
            sideways(blocks, hop, relay_rows).wait_send()
        place_copy.wait_send()
        spill_copy.wait_send()
        spill_back_copy.wait_send()

        @pl.loop(1, middle)
        def _(step):
            relay(step).wait_send()
            relay_home(step).wait_send()

        @pl.loop(1, groups)
        def _(step):
            send_count(step).wait()

        most_ref[...] = jnp.max(counts[...], axis=0)
    else:
        most_ref[...] = jnp.zeros_like(most_ref)
    for hop in range(1, parts):
        gate_copy(hop, part).wait_send()
        gate_copy(hop, lax.rem(part + parts - hop, parts)).wait_recv()
    result = gate_sums[0]
    for piece in range(1, parts):
        result = result + gate_sums[piece]
    gate_out_ref[...] = result[:1]


def call(groups, parts, capacity, spill, grad_out, hidden_in, ids, w_down):
    tokens, width = grad_out.shape
    units, features = w_down.shape
    tile = min(512, units)
    rows = groups * capacity * 3 // 4 if spill else groups * capacity
    dma = pltpu.SemaphoreType.DMA
    hops = max(parts - 1, 1)
    middle = groups // 2
    lanes = -(-spill // LANES) * LANES
    relayed = middle * capacity // 2
    extra = relayed if spill else 0
    spill_scratch = [
        pltpu.VMEM((tokens, LANES), jnp.int32),
        pltpu.VMEM((1, lanes), jnp.int32),
        pltpu.VMEM((1, lanes), jnp.int32),
        pltpu.VMEM((groups, 1, LANES), jnp.int32),
        pltpu.VMEM((spill, width), jnp.bfloat16),
        pltpu.VMEM((lanes, width), jnp.bfloat16),
        pltpu.VMEM((relayed, width), jnp.bfloat16),
        pltpu.VMEM((relayed, units), jnp.bfloat16),
        pltpu.VMEM((spill, units), jnp.bfloat16),
        pltpu.VMEM((lanes, units), jnp.bfloat16),
        dma((2,)),
        dma((groups,)),
        dma((groups,)),
        dma((2,)),
        dma((middle,)),
        dma((middle,)),
        dma((middle,)),
        dma((middle,)),
        dma((2,)),
    ]
    return pl.pallas_call(
        functools.partial(kernel, groups, parts, capacity, tile, spill),
        out_shape=(
            jax.ShapeDtypeStruct((tokens, units), jnp.bfloat16),
            jax.ShapeDtypeStruct((1, tokens), jnp.float32),
            jax.ShapeDtypeStruct((1, LANES), jnp.int32),
        ),
        in_specs=[
            pl.BlockSpec(memory_space=pl.ANY),
            pl.BlockSpec(memory_space=pl.ANY),
            pl.BlockSpec(memory_space=pltpu.VMEM),
            pl.BlockSpec(memory_space=pl.ANY),
        ],
        out_specs=(pl.BlockSpec(memory_space=pltpu.VMEM),) * 3,
        scratch_shapes=[
            pltpu.VMEM((tokens, width), jnp.bfloat16),
            pltpu.VMEM((tokens, units), jnp.bfloat16),
            pltpu.VMEM((units, features), jnp.bfloat16),
            pltpu.VMEM((rows, width), jnp.bfloat16),
            pltpu.VMEM((parts, rows + extra, width), jnp.bfloat16),
            pltpu.VMEM((rows + extra, units), jnp.bfloat16),
            pltpu.VMEM((rows, units), jnp.bfloat16),
            pltpu.VMEM((tokens, units), jnp.float32),
            pltpu.VMEM((1, tokens), jnp.int32),
            pltpu.VMEM((tokens, LANES), jnp.int32),
            pltpu.VMEM((tokens, LANES), jnp.float32),
            pltpu.VMEM((parts, 8, tokens), jnp.float32),
            dma((3,)),
            dma((groups,)),
            dma((groups,)),
            dma((hops, groups // 2 + 1)),
            dma((hops, groups // 2 + 1)),
            dma((groups,)),
            dma((groups,)),
            dma((hops,)),
            dma((hops,)),
        ]
        + (spill_scratch if spill else []),
        compiler_params=pltpu.CompilerParams(
            collective_id=1 if spill else 0,
            has_side_effects=True,
            vmem_limit_bytes=56 * 1024 * 1024,
        ),
    )(grad_out, hidden_in, ids, w_down)


def body(groups, parts, grad_out, hidden_in, gate_prob, expert_ids, w_down):
    tokens = grad_out.shape[0]
    experts, units, features = w_down.shape
    capacity = 2 * tokens // (groups * experts)
    args = (grad_out, hidden_in, expert_ids.reshape(1, tokens), w_down.reshape(units, features))
    whole = functools.partial(call, groups, parts, capacity, 0)
    spill = 9 * groups * capacity // 64 // 16 * 16
    if capacity % 32 == 0:
        back, gate_sum, most = call(groups, parts, capacity, spill, *args)
        back, gate_sum = lax.cond(
            most[0, 0] > spill,
            lambda back, gate_sum: whole(*args)[:2],
            lambda back, gate_sum: (back, gate_sum),
            back,
            gate_sum,
        )
    else:
        back, gate_sum, _ = whole(*args)
    grad_hidden = (gate_prob[:, None] * back.astype(jnp.float32)).astype(jnp.bfloat16)
    return grad_hidden, gate_sum.reshape(tokens)


def solution(mesh):
    return jax.shard_map(
        functools.partial(body, mesh.shape["expert"], mesh.shape["tensor"]),
        mesh=mesh,
        in_specs=(
            P("expert", "tensor"),
            P("expert", "tensor"),
            P("expert"),
            P("expert", None),
            P("expert", "tensor", None),
        ),
        out_specs=(P("expert", "tensor"), P("expert")),
        check_vma=False,
    )
```

```python
import functools

import jax
import jax.numpy as jnp
from jax import lax
from jax.experimental import pallas as pl
from jax.experimental.pallas import tpu as pltpu
from jax.sharding import PartitionSpec as P

MESH = pl.DeviceIdType.MESH
LANES = 128
FAR = "far"


def across(index, step, count):
    total, bit = 0, 1
    while bit < count:
        total = total + lax.rem(lax.div(index, bit) + lax.div(step, bit), 2) * bit
        bit *= 2
    return total


def steps_of(pair, groups):
    quarter = groups // 4
    near = jnp.where(pair < quarter, quarter + pair, lax.rem(pair + 1, quarter))
    return groups // 2 + pair, near


def tiled_lanes(column, width):
    return jnp.concatenate([column] * (width // LANES), axis=1)


def kernel(
    groups,
    parts,
    capacity,
    tile,
    spill,
    grad_ref,
    hidden_ref,
    ids_ref,
    w_ref,
    out_ref,
    gate_out_ref,
    most_ref,
    grad,
    hidden,
    weight,
    outgoing,
    arrived,
    product,
    returned,
    total,
    slot_row,
    slot_column,
    sums,
    gate_sums,
    local_sem,
    send_sem,
    recv_sem,
    peer_send_sem,
    peer_recv_sem,
    back_send_sem,
    back_recv_sem,
    gate_send_sem,
    gate_recv_sem,
    *spill_refs,
):
    me = lax.axis_index("expert")
    part = lax.axis_index("tensor")
    pairs = groups // 2
    tokens, width = grad.shape
    units = weight.shape[0]
    middle = groups // 2
    half = capacity // 2
    side = lax.div(me, middle)
    local = me - side * middle
    if spill:
        (
            spill_column,
            place_out,
            place_in,
            counts,
            spill_out,
            spill_in,
            relay_out,
            relay_back,
            spill_back,
            spill_home,
            place_sem,
            count_send_sem,
            count_recv_sem,
            spill_sem,
            relay_send_sem,
            relay_recv_sem,
            relay_back_send_sem,
            relay_back_recv_sem,
            spill_back_sem,
        ) = spill_refs
        lanes = place_in.shape[1]
    far_rows = half if spill else capacity
    both = far_rows + capacity
    relayed = middle * half

    load_grad = pltpu.make_async_copy(grad_ref, grad, local_sem.at[0])
    load_weight = pltpu.make_async_copy(w_ref, weight, local_sem.at[1])
    load_hidden = pltpu.make_async_copy(hidden_ref, hidden, local_sem.at[2])
    load_grad.start()
    load_weight.start()
    load_hidden.start()

    barrier = pltpu.get_barrier_semaphore()

    @pl.loop(1, groups)
    def _(step):
        pl.semaphore_signal(
            barrier, inc=1, device_id=(across(me, step, groups), part), device_id_type=MESH
        )

    for hop in range(1, parts):
        pl.semaphore_signal(
            barrier, inc=1, device_id=(me, lax.rem(part + hop, parts)), device_id_type=MESH
        )

    ids = ids_ref[...]
    ids_column = jnp.broadcast_to(ids, (LANES, tokens)).T
    earlier = jnp.zeros((1, tokens), jnp.int32)
    for start in range(0, tokens, LANES):
        rows = min(LANES, tokens - start)
        shape = (rows, tokens)
        same = tiled_lanes(ids_column[start : start + rows], tokens) == ids
        before = lax.broadcasted_iota(jnp.int32, shape, 0) + start < lax.broadcasted_iota(
            jnp.int32, shape, 1
        )
        earlier = earlier + jnp.sum(
            jnp.where(same & before, 1, 0), axis=0, keepdims=True
        )
    slots = ids * capacity + earlier
    slot_row[...] = slots
    slot_column[...] = jnp.broadcast_to(slots, (LANES, tokens)).T
    load_grad.wait()

    def rows_of(pair):
        return pl.ds(pl.multiple_of(pair * both, 16), both)

    def pack(pair, target):
        far, near = steps_of(pair, groups)
        chosen = []
        for step, size in ((far, far_rows), (near, capacity)):
            row = lax.broadcasted_iota(jnp.int32, (size, tokens), 0)
            wanted = row + across(me, step, groups) * capacity
            chosen.append(jnp.where(slot_row[...] == wanted, 1.0, 0.0))
        pick = jnp.concatenate(chosen, axis=0).astype(jnp.bfloat16)
        rows = jnp.dot(pick, grad[...], preferred_element_type=jnp.float32)
        target[rows_of(pair), :] = rows.astype(jnp.bfloat16)

    def sent_rows(slot, kind):
        pair = lax.div(slot, 2)
        if kind is FAR:
            return pl.ds(pl.multiple_of(pair * both, 16), far_rows)
        return pl.ds(pl.multiple_of(pair * both + far_rows, 16), capacity)

    def outward(slot, step, kind=None):
        return pltpu.make_async_remote_copy(
            src_ref=outgoing.at[sent_rows(slot, kind)],
            dst_ref=arrived.at[part, sent_rows(slot, kind)],
            send_sem=send_sem.at[slot],
            recv_sem=recv_sem.at[slot],
            device_id=(across(me, step, groups), part),
            device_id_type=MESH,
        )

    def sideways(pair, hop, rows=None):
        rows = rows_of(pair) if rows is None else rows
        return pltpu.make_async_remote_copy(
            src_ref=arrived.at[part, rows],
            dst_ref=arrived.at[part, rows],
            send_sem=peer_send_sem.at[hop - 1, pair],
            recv_sem=peer_recv_sem.at[hop - 1, pair],
            device_id=(me, lax.rem(part + hop, parts)),
            device_id_type=MESH,
        )

    def sideways_in(pair, hop, rows=None):
        rows = rows_of(pair) if rows is None else rows
        sender = lax.rem(part + parts - hop, parts)
        return pltpu.make_async_remote_copy(
            src_ref=arrived.at[sender, rows],
            dst_ref=arrived.at[sender, rows],
            send_sem=peer_send_sem.at[hop - 1, pair],
            recv_sem=peer_recv_sem.at[hop - 1, pair],
            device_id=(me, lax.rem(part + hop, parts)),
            device_id_type=MESH,
        )

    def homeward(slot, step, kind=None):
        return pltpu.make_async_remote_copy(
            src_ref=product.at[sent_rows(slot, kind)],
            dst_ref=returned.at[sent_rows(slot, kind)],
            send_sem=back_send_sem.at[slot],
            recv_sem=back_recv_sem.at[slot],
            device_id=(across(me, step, groups), part),
            device_id_type=MESH,
        )

    own = pairs - 1
    own_rows = pl.ds(own * both + far_rows, capacity)

    def send_pair(pair):
        far, near = steps_of(pair, groups)
        outward(2 * pair, far, FAR).start()

        @pl.when(pair < own)
        def _():
            outward(2 * pair + 1, near).start()

    if spill:
        mirror = (across(me, middle, groups), part)

        def to_mirror(source, target, sems):
            return pltpu.make_async_remote_copy(
                src_ref=source,
                dst_ref=target,
                send_sem=sems.at[0],
                recv_sem=sems.at[1],
                device_id=mirror,
                device_id_type=MESH,
            )

        def send_count(step):
            return pltpu.make_async_remote_copy(
                src_ref=counts.at[0],
                dst_ref=counts.at[step],
                send_sem=count_send_sem.at[step],
                recv_sem=count_recv_sem.at[step],
                device_id=(across(me, step, groups), part),
                device_id_type=MESH,
            )

        def half_rows(index):
            return pl.ds(pl.multiple_of(index * half, half), half)

        relay_rows = pl.ds(pairs * both, relayed)
        own_relay = pl.ds(pairs * both, half)

        def relay_at(step):
            return pl.ds(pl.multiple_of(pairs * both + step * half, 16), half)

        def relay(step):
            target = across(me, step, groups)
            return pltpu.make_async_remote_copy(
                src_ref=relay_out.at[half_rows(target - side * middle)],
                dst_ref=arrived.at[part, relay_at(step)],
                send_sem=relay_send_sem.at[step],
                recv_sem=relay_recv_sem.at[step],
                device_id=(target, part),
                device_id_type=MESH,
            )

        def relay_home(step):
            return pltpu.make_async_remote_copy(
                src_ref=product.at[relay_at(step)],
                dst_ref=relay_back.at[half_rows(local)],
                send_sem=relay_back_send_sem.at[step],
                recv_sem=relay_back_recv_sem.at[step],
                device_id=(across(me, step, groups), part),
                device_id_type=MESH,
            )

        def relay_home_in(step):
            sender = across(me, step, groups) - side * middle
            return pltpu.make_async_remote_copy(
                src_ref=product.at[relay_at(step)],
                dst_ref=relay_back.at[half_rows(sender)],
                send_sem=relay_back_send_sem.at[step],
                recv_sem=relay_back_recv_sem.at[step],
                device_id=(across(me, step, groups), part),
                device_id_type=MESH,
            )

        place_copy = to_mirror(place_out, place_in, place_sem)
        spill_copy = to_mirror(spill_out, spill_in.at[pl.ds(0, spill)], spill_sem)
        spill_back_copy = to_mirror(
            spill_back, spill_home.at[pl.ds(0, spill)], spill_back_sem
        )
        early = 5 * pairs // 8
        pack(0, outgoing)
        pl.semaphore_wait(barrier, groups - 1 + parts - 1)
        send_pair(0)
        expert_side = jnp.where(ids >= middle, 1, 0)
        over = jnp.where((expert_side != side) & (earlier >= half), 1, 0)
        over_column = jnp.broadcast_to(over, (LANES, tokens)).T
        order = jnp.zeros((1, tokens), jnp.int32)
        for start in range(0, tokens, LANES):
            rows = min(LANES, tokens - start)
            shape = (rows, tokens)
            before = lax.broadcasted_iota(jnp.int32, shape, 0) + start < lax.broadcasted_iota(
                jnp.int32, shape, 1
            )
            ahead = tiled_lanes(over_column[start : start + rows], tokens)
            order = order + jnp.sum(jnp.where(before, ahead, 0), axis=0, keepdims=True)
        order = jnp.where(over > 0, order, -1)
        spill_column[...] = jnp.broadcast_to(order, (LANES, tokens)).T
        spot = (ids - expert_side * middle) * half + earlier - half + 1
        spot_column = jnp.broadcast_to(spot, (LANES, tokens)).T
        match = tiled_lanes(spill_column[...], lanes) == lax.broadcasted_iota(
            jnp.int32, (tokens, lanes), 1
        )
        place_out[...] = (
            jnp.sum(
                jnp.where(match, tiled_lanes(spot_column, lanes), 0), axis=0, keepdims=True
            )
            - 1
        )
        counts[0] = jnp.broadcast_to(jnp.sum(over, axis=1, keepdims=True), (1, LANES))
        spill_in[spill:, :] = jnp.zeros((lanes - spill, width), jnp.bfloat16)
        spill_home[spill:, :] = jnp.zeros((lanes - spill, units), jnp.bfloat16)
        index = lax.broadcasted_iota(jnp.int32, (spill, tokens), 0)
        pick = jnp.where(order == index, 1.0, 0.0).astype(jnp.bfloat16)
        spill_out[...] = jnp.dot(
            pick, grad[...], preferred_element_type=jnp.float32
        ).astype(jnp.bfloat16)
        place_copy.start()
        spill_copy.start()

        @pl.loop(1, max(early, 1))
        def _(pair):
            pack(pair, outgoing)
            send_pair(pair)

        place_copy.wait_recv()
        spill_copy.wait_recv()
        index = lax.broadcasted_iota(jnp.int32, (relayed, lanes), 0)
        pick = jnp.where(place_in[...] == index, 1.0, 0.0).astype(jnp.bfloat16)
        relay_out[...] = jnp.dot(
            pick, spill_in[...], preferred_element_type=jnp.float32
        ).astype(jnp.bfloat16)

        @pl.loop(1, middle)
        def _(step):
            relay(step).start()

        arrived[part, own_relay, :] = relay_out[half_rows(local), :]

        @pl.loop(max(early, 1), pairs)
        def _(pair):
            pack(pair, outgoing)
            send_pair(pair)

        @pl.loop(1, groups)
        def _(step):
            send_count(step).start()

    else:
        pack(0, outgoing)
        pl.semaphore_wait(barrier, groups - 1 + parts - 1)
        send_pair(0)

        @pl.loop(1, pairs)
        def _(pair):
            pack(pair, outgoing)
            send_pair(pair)

    arrived[part, own_rows, :] = outgoing[own_rows, :]

    def multiply(rows):
        @pl.loop(0, units // tile)
        def _(block):
            columns = pl.ds(pl.multiple_of(block * tile, tile), tile)
            value = jnp.zeros((rows.size, tile), jnp.float32)
            for piece in range(parts):
                value = value + lax.dot_general(
                    arrived[piece, rows, :],
                    weight[columns, piece * width : (piece + 1) * width],
                    (((1,), (1,)), ((), ())),
                    preferred_element_type=jnp.float32,
                )
            product[rows, columns] = value.astype(jnp.bfloat16)

    if spill:

        def multiply_relayed():
            @pl.loop(1, middle)
            def _(step):
                relay(step).wait_recv()

            for hop in range(1, parts):
                sideways(pairs, hop, relay_rows).start()
            for hop in range(1, parts):
                sideways_in(pairs, hop, relay_rows).wait_recv()
            multiply(relay_rows)

            @pl.loop(1, middle)
            def _(step):
                relay_home(step).start()

        def pack_home():
            relay_back[half_rows(local), :] = product[own_relay, :]

            @pl.loop(1, middle)
            def _(step):
                relay_home_in(step).wait_recv()

            column = jnp.broadcast_to(place_in[...], (LANES, lanes)).T[:spill]
            index = lax.broadcasted_iota(jnp.int32, (spill, relayed), 1)
            wide = jnp.concatenate([column] * -(-relayed // LANES), axis=1)
            pick = jnp.where(wide[:, : relayed] == index, 1.0, 0.0).astype(jnp.bfloat16)

            @pl.loop(0, units // tile)
            def _(block):
                columns = pl.ds(pl.multiple_of(block * tile, tile), tile)
                spill_back[:, columns] = jnp.dot(
                    pick, relay_back[:, columns], preferred_element_type=jnp.float32
                ).astype(jnp.bfloat16)

            spill_back_copy.start()

    @pl.loop(0, pairs + 1)
    def _(turn):
        @pl.when(turn < pairs)
        def _():
            far, near = steps_of(turn, groups)
            outward(2 * turn, far, FAR).wait_recv()

            @pl.when(turn < own)
            def _():
                outward(2 * turn + 1, near).wait_recv()

            for hop in range(1, parts):
                sideways(turn, hop).start()

        @pl.when(turn == 0)
        def _():
            load_weight.wait()

        @pl.when(turn > 0)
        def _():
            pair = turn - 1
            for hop in range(1, parts):
                sideways_in(pair, hop).wait_recv()
            multiply(rows_of(pair))
            far, near = steps_of(pair, groups)
            homeward(2 * pair, far, FAR).start()

            @pl.when(pair < own)
            def _():
                homeward(2 * pair + 1, near).start()

        if spill:

            @pl.when(turn == max(early, 1))
            def _():
                multiply_relayed()

            @pl.when(turn == own)
            def _():
                pack_home()

    returned[own_rows, :] = product[own_rows, :]
    load_hidden.wait()
    total[...] = jnp.zeros_like(total)
    sums[...] = jnp.zeros_like(sums)

    def placement(pair, rows):
        far, near = steps_of(pair, groups)
        lane = lax.broadcasted_iota(jnp.int32, (1, both), 1)
        wanted = jnp.where(
            lane < far_rows,
            lane + across(me, far, groups) * capacity,
            lane + across(me, near, groups) * capacity - far_rows,
        )
        hit = slot_column[rows, :both] == wanted
        return jnp.where(hit, 1.0, 0.0).astype(jnp.bfloat16)

    def wait_home(pair):
        far, near = steps_of(pair, groups)
        homeward(2 * pair, far, FAR).wait_recv()

        @pl.when(pair < own)
        def _():
            homeward(2 * pair + 1, near).wait_recv()

    everything = pl.ds(0, tokens)

    def gather(place, source, rows):
        @pl.loop(0, units // tile)
        def _(block):
            columns = pl.ds(pl.multiple_of(block * tile, tile), tile)
            total[:, columns] += jnp.dot(
                place, source[rows, columns], preferred_element_type=jnp.float32
            )

    @pl.loop(0, own)
    def _(pair):
        wait_home(pair)
        gather(placement(pair, everything), returned, rows_of(pair))

    if spill:
        spill_back_copy.wait_recv()
        lane = lax.broadcasted_iota(jnp.int32, (tokens, lanes), 1)
        hit = tiled_lanes(spill_column[...], lanes) == lane
        gather(jnp.where(hit, 1.0, 0.0).astype(jnp.bfloat16), spill_home, pl.ds(0, lanes))
    wait_home(own)
    chunk = min(LANES, tokens)

    @pl.loop(0, tokens // chunk)
    def _(part_of):
        rows = pl.ds(pl.multiple_of(part_of * chunk, chunk), chunk)
        place = placement(own, rows)

        @pl.loop(0, units // tile)
        def _(block):
            columns = pl.ds(pl.multiple_of(block * tile, tile), tile)
            back = total[rows, columns] + jnp.dot(
                place, returned[rows_of(own), columns], preferred_element_type=jnp.float32
            )
            out_ref[rows, columns] = back.astype(jnp.bfloat16)
            terms = hidden[rows, columns].astype(jnp.float32) * back
            sums[rows, :] += sum(
                terms[:, at : at + LANES] for at in range(0, tile, LANES)
            )

    row = jnp.sum(sums[...].T, axis=0, keepdims=True)
    gate_sums[part] = jnp.broadcast_to(row, (8, tokens))

    def gate_copy(hop, sender):
        return pltpu.make_async_remote_copy(
            src_ref=gate_sums.at[sender],
            dst_ref=gate_sums.at[sender],
            send_sem=gate_send_sem.at[hop - 1],
            recv_sem=gate_recv_sem.at[hop - 1],
            device_id=(me, lax.rem(part + hop, parts)),
            device_id_type=MESH,
        )

    for hop in range(1, parts):
        gate_copy(hop, part).start()

    @pl.loop(0, pairs)
    def _(pair):
        far, near = steps_of(pair, groups)
        outward(2 * pair, far, FAR).wait_send()
        homeward(2 * pair, far, FAR).wait_send()
        for hop in range(1, parts):
            sideways(pair, hop).wait_send()

        @pl.when(pair < own)
        def _():
            outward(2 * pair + 1, near).wait_send()
            homeward(2 * pair + 1, near).wait_send()

    if spill:
        for hop in range(1, parts):
            sideways(pairs, hop, relay_rows).wait_send()
        place_copy.wait_send()
        spill_copy.wait_send()
        spill_back_copy.wait_send()

        @pl.loop(1, middle)
        def _(step):
            relay(step).wait_send()
            relay_home(step).wait_send()

        @pl.loop(1, groups)
        def _(step):
            send_count(step).wait()

        most_ref[...] = jnp.max(counts[...], axis=0)
    else:
        most_ref[...] = jnp.zeros_like(most_ref)
    for hop in range(1, parts):
        gate_copy(hop, part).wait_send()
        gate_copy(hop, lax.rem(part + parts - hop, parts)).wait_recv()
    result = gate_sums[0]
    for piece in range(1, parts):
        result = result + gate_sums[piece]
    gate_out_ref[...] = result[:1]


def call(groups, parts, capacity, spill, grad_out, hidden_in, ids, w_down):
    tokens, width = grad_out.shape
    units, features = w_down.shape
    tile = min(512, units)
    rows = groups * capacity * 3 // 4 if spill else groups * capacity
    dma = pltpu.SemaphoreType.DMA
    hops = max(parts - 1, 1)
    middle = groups // 2
    lanes = -(-spill // LANES) * LANES
    relayed = middle * capacity // 2
    extra = relayed if spill else 0
    spill_scratch = [
        pltpu.VMEM((tokens, LANES), jnp.int32),
        pltpu.VMEM((1, lanes), jnp.int32),
        pltpu.VMEM((1, lanes), jnp.int32),
        pltpu.VMEM((groups, 1, LANES), jnp.int32),
        pltpu.VMEM((spill, width), jnp.bfloat16),
        pltpu.VMEM((lanes, width), jnp.bfloat16),
        pltpu.VMEM((relayed, width), jnp.bfloat16),
        pltpu.VMEM((relayed, units), jnp.bfloat16),
        pltpu.VMEM((spill, units), jnp.bfloat16),
        pltpu.VMEM((lanes, units), jnp.bfloat16),
        dma((2,)),
        dma((groups,)),
        dma((groups,)),
        dma((2,)),
        dma((middle,)),
        dma((middle,)),
        dma((middle,)),
        dma((middle,)),
        dma((2,)),
    ]
    return pl.pallas_call(
        functools.partial(kernel, groups, parts, capacity, tile, spill),
        out_shape=(
            jax.ShapeDtypeStruct((tokens, units), jnp.bfloat16),
            jax.ShapeDtypeStruct((1, tokens), jnp.float32),
            jax.ShapeDtypeStruct((1, LANES), jnp.int32),
        ),
        in_specs=[
            pl.BlockSpec(memory_space=pl.ANY),
            pl.BlockSpec(memory_space=pl.ANY),
            pl.BlockSpec(memory_space=pltpu.VMEM),
            pl.BlockSpec(memory_space=pl.ANY),
        ],
        out_specs=(pl.BlockSpec(memory_space=pltpu.VMEM),) * 3,
        scratch_shapes=[
            pltpu.VMEM((tokens, width), jnp.bfloat16),
            pltpu.VMEM((tokens, units), jnp.bfloat16),
            pltpu.VMEM((units, features), jnp.bfloat16),
            pltpu.VMEM((rows, width), jnp.bfloat16),
            pltpu.VMEM((parts, rows + extra, width), jnp.bfloat16),
            pltpu.VMEM((rows + extra, units), jnp.bfloat16),
            pltpu.VMEM((rows, units), jnp.bfloat16),
            pltpu.VMEM((tokens, units), jnp.float32),
            pltpu.VMEM((1, tokens), jnp.int32),
            pltpu.VMEM((tokens, LANES), jnp.int32),
            pltpu.VMEM((tokens, LANES), jnp.float32),
            pltpu.VMEM((parts, 8, tokens), jnp.float32),
            dma((3,)),
            dma((groups,)),
            dma((groups,)),
            dma((hops, groups // 2 + 1)),
            dma((hops, groups // 2 + 1)),
            dma((groups,)),
            dma((groups,)),
            dma((hops,)),
            dma((hops,)),
        ]
        + (spill_scratch if spill else []),
        compiler_params=pltpu.CompilerParams(
            collective_id=1 if spill else 0,
            has_side_effects=True,
            vmem_limit_bytes=56 * 1024 * 1024,
        ),
    )(grad_out, hidden_in, ids, w_down)


def body(groups, parts, grad_out, hidden_in, gate_prob, expert_ids, w_down):
    tokens = grad_out.shape[0]
    experts, units, features = w_down.shape
    capacity = 2 * tokens // (groups * experts)
    args = (grad_out, hidden_in, expert_ids.reshape(1, tokens), w_down.reshape(units, features))
    whole = functools.partial(call, groups, parts, capacity, 0)
    spill = 9 * groups * capacity // 64 // 16 * 16
    if capacity % 32 == 0:
        back, gate_sum, most = call(groups, parts, capacity, spill, *args)
        back, gate_sum = lax.cond(
            most[0, 0] > spill,
            lambda back, gate_sum: whole(*args)[:2],
            lambda back, gate_sum: (back, gate_sum),
            back,
            gate_sum,
        )
    else:
        back, gate_sum, _ = whole(*args)
    grad_hidden = (gate_prob[:, None] * back.astype(jnp.float32)).astype(jnp.bfloat16)
    return grad_hidden, gate_sum.reshape(tokens)


def solution(mesh):
    return jax.shard_map(
        functools.partial(body, mesh.shape["expert"], mesh.shape["tensor"]),
        mesh=mesh,
        in_specs=(
            P("expert", "tensor"),
            P("expert", "tensor"),
            P("expert"),
            P("expert", None),
            P("expert", "tensor", None),
        ),
        out_specs=(P("expert", "tensor"), P("expert")),
        check_vma=False,
    )
```
